128 devices in a mesh: rep: 8 (over y_hi, z), shard: 16 (over y_lo, x, core).
Axes of the slice: x: 4, y: 4 (y_hi: 2, y_lo: 2; y = y_hi * 2 + y_lo), z: 4, core: 2. Of those that a mesh axis runs over, the one named last changes fastest.
Arguments:
- block_input: bfloat16 [32768, 1024], P(('rep', 'shard')), may hold values from -6 to 6
- cotangent: bfloat16 [32768, 1024], P(('rep', 'shard')), may hold values from -6 to 6
- routes: int32 [32768, 8], P(('rep', 'shard')), may hold values from 0 to 31, all different within a row; in each aligned block of 128 rows (0 to 127, 128 to 255, ...) at most 44 rows name the same one
- lengths: int32 [8, 2, 8], P('rep'), may hold values from 1 to 1024, 2048 in all within a row
- stream_slot: int32 [8, 2, 2048], P('rep'), may hold values from 0 to 2047, as said below
- w_qkv: bfloat16 [1024, 2048], P('shard'), may hold values from -0.1875 to 0.1875
- w_out: bfloat16 [1024, 1024], P('shard'), may hold values from -0.375 to 0.375
- w_router: bfloat16 [1024, 32], P('shard'), may hold values from -0.09375 to 0.09375
- g_attn: bfloat16 [1024], P('shard'), may hold values from 0.25 to 1.75
- g_moe: bfloat16 [1024], P('shard'), may hold values from 0.25 to 1.75
- g_q: bfloat16 [64], P('shard'), may hold values from 0.25 to 1.75
- g_k: bfloat16 [64], P('shard'), may hold values from 0.25 to 1.75
- w_gate: bfloat16 [32, 1024, 512], P('shard'), may hold values from -0.1875 to 0.1875
- w_up: bfloat16 [32, 1024, 512], P('shard'), may hold values from -0.1875 to 0.1875
- w_down: bfloat16 [32, 512, 1024], P('shard'), may hold values from -0.5 to 0.5
Outputs:
- mixed: bfloat16 [32768, 1024], P(('rep', 'shard'))
- grad_input: bfloat16 [32768, 1024], P(('rep', 'shard'))
- grad_qkv: float32 [1024, 2048], P('shard')
- grad_out: float32 [1024, 1024], P('shard')
- grad_router: float32 [1024, 32], P('shard')
- grad_attn_gain: float32 [1024], P('shard')
- grad_moe_gain: float32 [1024], P('shard')
- grad_q_gain: float32 [64], P('shard')
- grad_k_gain: float32 [64], P('shard')
- grad_gate: float32 [32, 1024, 512], P('shard')
- grad_up: float32 [32, 1024, 512], P('shard')
- grad_down: float32 [32, 512, 1024], P('shard')
The draws below stay inside these ranges and needn't reach their ends.
Inputs may be any that keep to these rules, and one draw needn't show every extreme that they name: `routes`: in each aligned block of 128 rows (the rows of one device in one micro-batch) no expert is named more than 44 times, a bound that some block reaches; a row names 8 different experts. Each row of 8 lengths sums to 2048; its longest is 1024. `stream_slot`: for each group and micro-batch the 2048 entries are a permutation of the stream positions.
All inputs are finite; a program needn't handle non-finite values.
Results may differ from the reference program's by a relative error of at most 0.019.
Values may be sent and summed in bfloat16 or wider, within the bound.
No kernel may reach another device: no remote copies, remote signals or barrier semaphores. Data moves between devices by JAX's collectives and lax.ppermute only.
A program may use at most 256 MiB of HBM per device.

```python
import math
import jax
import jax.numpy as jnp
import numpy as np
from jax import lax

D = 1024
HEADS = 16
KV_HEADS = 8
HD = 64
FF = 512
TOP = 8
MICRO = 2
SEQS = 8
TPD = 128
EXPERTS = 32
G = 2048
TOKENS = 32768
MOST = 1024
CAP = 44
N_REP = 8
N_SHARD = 16


def draw_stream_slot(key, part):
    key = jax.random.fold_in(key, 7)
    shift_key, order_key = jax.random.split(key)
    shifts = jax.random.randint(shift_key, (N_REP, MICRO, 1, 1), 0, N_SHARD)
    order_keys = jax.random.split(order_key, N_REP * MICRO * N_SHARD)

    def one_order(single_key):
        return jax.random.permutation(single_key, TPD)
    orders = jax.vmap(one_order)(order_keys).reshape(N_REP, MICRO, N_SHARD, TPD)
    device = jnp.arange(N_SHARD).reshape(1, 1, N_SHARD, 1)
    first = (device - shifts) % N_SHARD
    return (first + N_SHARD * orders).reshape(N_REP, MICRO, N_SHARD * TPD).astype(jnp.int32)


def levels(own_key, shape, cuts, low, high):
    loudness = 1.0
    for dim, blocks in cuts:
        heights = jax.random.uniform(jax.random.fold_in(jax.random.fold_in(own_key, 6), dim), (blocks,), jnp.float32, low / len(cuts), high / len(cuts))
        loudness = loudness * jnp.repeat(jnp.exp(heights), shape[dim] // blocks).reshape((-1,) + (1,) * (len(shape) - 1 - dim))
    return loudness


def length_profile(amount, total, reach, skew):
    weights = [(1 << 20) // math.isqrt(rank ** skew) + 1 for rank in range(2, amount + 1)]
    surplus, given = total - reach - (amount - 1), [1] * (amount - 1)
    while surplus > 0:
        candidates = [i for i in range(amount - 1) if given[i] < reach]
        whole, budget = sum([weights[i] for i in candidates]), surplus
        for i in candidates:
            addition = min(reach - given[i], max(1, budget * weights[i] // whole), surplus)
            given[i] = given[i] + addition
            surplus = surplus - addition
    return np.array([reach] + given)


def uneven_parts(key, amount, total, most, skew):
    if amount == 2:
        one = jax.random.randint(key, (), max(1, total - most), min(most, total - 1) + 1)
        return jnp.stack([one, total - one])
    sizes = jnp.asarray(length_profile(amount, total, most, skew), jnp.int32)
    couples = (amount - 1) // 2
    donor, receiver = sizes[1:1 + 2 * couples:2], sizes[2:2 + 2 * couples:2]
    room = jnp.minimum(donor - 1, most - receiver)
    moved = jax.random.randint(jax.random.fold_in(key, 1), (couples,), 0, 1 << 20) % (room + 1)
    sizes = sizes.at[1:1 + 2 * couples:2].set(donor - moved).at[2:2 + 2 * couples:2].set(receiver + moved)
    return sizes[jax.random.permutation(jax.random.fold_in(key, 2), amount)]


def routed_block(stream_key, own, number, rows, number_of, top, bound, skew):
    ranking = jax.random.permutation(stream_key, number_of)
    packed, common = portions_of(number_of, rows * top, bound, skew, True), portions_of(number_of, rows * top, bound, skew, False)
    places = jnp.arange(number_of)

    def named(tallies, rotation):
        used = int((tallies > 0).sum())
        fixed = max(1, used // 4)
        moved = fixed + (places - fixed + rotation * (used - fixed)) % max(1, number_of - fixed)
        return jnp.zeros((number_of,), jnp.int32).at[ranking[jnp.where(places < fixed, places, moved)]].set(jnp.asarray(tallies, jnp.int32))

    tallies = jnp.where(number % 4 == 0, named(packed, number // 4), named(common, number - number // 4 - 1))
    mixed = jax.random.permutation(jax.random.fold_in(own, 3), number_of)
    giver, receiver = mixed[0:number_of // 2 * 2:2], mixed[1:number_of // 2 * 2:2]
    slack = jnp.minimum(tallies[giver] - 1, bound - tallies[receiver]) // 2
    slack = jnp.where((giver == ranking[0]) | (receiver == ranking[0]) | (tallies[receiver] == 0), 0, jnp.maximum(slack, 0))
    moved = jax.random.randint(jax.random.fold_in(own, 4), (number_of // 2,), 0, 1 << 20) % (slack + 1)
    tallies = tallies.at[giver].add(-moved).at[receiver].add(moved)
    members = jnp.searchsorted(jnp.cumsum(tallies), jnp.arange(rows * top), side="right").astype(jnp.int32)
    grid = members.reshape(top, rows).T
    grid = grid[jax.random.permutation(jax.random.fold_in(own, 1), rows)]
    rotation = jax.random.randint(jax.random.fold_in(own, 2), (rows, 1), 0, top)
    return jnp.take_along_axis(grid, (jnp.arange(top)[None, :] + rotation) % top, axis=1)


def portions_of(amount, total, most, slope, full):
    portions = [(1 << 20) // math.isqrt(standing ** slope) + 1 for standing in range(1, amount + 1)]
    largest = most if full else min(most, max(-(-total // amount), total * portions[0] // sum(portions)))
    least = 1 if total - largest >= amount - 1 else 0
    holding, rest = [largest] + [least] * (amount - 1), total - largest - least * (amount - 1)
    while rest > 0:
        movable = [i for i in range(1, amount) if holding[i] < largest] or [i for i in range(1, amount) if holding[i] < most]
        mass, budget = sum([portions[i] for i in movable]), rest
        for i in movable:
            more = min(most - holding[i], max(1, budget * portions[i] // mass), rest)
            holding[i] = holding[i] + more
            rest = rest - more
    return np.array(holding)


def scatter_about(stream_key, dims, width, limit, pieces=(), kind=jnp.bfloat16):
    level = levels(stream_key, dims, pieces, -0.22, 0.18) if pieces else 1.0
    drawn = jax.random.normal(stream_key, dims, jnp.float32) * width * level
    return jnp.minimum(jnp.maximum(drawn, -limit), limit).astype(kind)


def setup_inputs(seed: int = 0) -> dict:
    key_list = jax.random.split(jax.random.key(seed), 16)
    block_input = scatter_about(key_list[0], (TOKENS, D), 1.0, 6.0, ((0, 128),))
    cotangent = scatter_about(key_list[1], (TOKENS, D), 1.0, 6.0, ((0, 128),))
    routes_keys = jax.random.split(jax.random.fold_in(key_list[2], 1), TOKENS // TPD)
    routes_turns = jax.random.permutation(jax.random.fold_in(key_list[2], 3), TOKENS // TPD)
    routes = jax.vmap(lambda own, number: routed_block(jax.random.fold_in(key_list[2], 2), own, number, TPD, EXPERTS, TOP, CAP, 2))(routes_keys, routes_turns).reshape((TOKENS, TOP))
    lengths = jax.vmap(lambda own: uneven_parts(own, SEQS, G, MOST, 2))(jax.random.split(key_list[3], N_REP * MICRO)).reshape((N_REP, MICRO, SEQS)).astype(jnp.int32)
    stream_slot = draw_stream_slot(jax.random.fold_in(key_list[15], 71), 0)
    w_qkv = scatter_about(key_list[5], (D, HEADS * HD + 2 * KV_HEADS * HD), D ** -0.5, 0.1875, ((0, 16),))
    w_out = scatter_about(key_list[6], (HEADS * HD, D), (4 * HD) ** -0.5, 0.375, ((0, 16),))
    w_router = scatter_about(key_list[7], (D, EXPERTS), (4 * D) ** -0.5, 0.09375, ((0, 16),))
    g_attn = jnp.clip(1.0 + 0.15 * jax.random.normal(key_list[8], (D,), jnp.float32), 0.25, 1.75).astype(jnp.bfloat16)
    g_moe = jnp.clip(1.0 + 0.15 * jax.random.normal(key_list[9], (D,), jnp.float32), 0.25, 1.75).astype(jnp.bfloat16)
    g_q = jnp.clip(1.0 + 0.15 * jax.random.normal(key_list[10], (HD,), jnp.float32), 0.25, 1.75).astype(jnp.bfloat16)
    g_k = jnp.clip(1.0 + 0.15 * jax.random.normal(key_list[11], (HD,), jnp.float32), 0.25, 1.75).astype(jnp.bfloat16)
    w_gate = scatter_about(key_list[12], (EXPERTS, D, FF), D ** -0.5, 0.1875, ((0, 16),))
    w_up = scatter_about(key_list[13], (EXPERTS, D, FF), D ** -0.5, 0.1875, ((0, 16),))
    w_down = scatter_about(key_list[14], (EXPERTS, FF, D), (FF // 4) ** -0.5, 0.5, ((0, 16),))
    return {"block_input": block_input, "cotangent": cotangent, "routes": routes, "lengths": lengths, "stream_slot": stream_slot, "w_qkv": w_qkv, "w_out": w_out, "w_router": w_router, "g_attn": g_attn, "g_moe": g_moe, "g_q": g_q, "g_k": g_k, "w_gate": w_gate, "w_up": w_up, "w_down": w_down}


@jax.custom_vjp
def low(v):
    return lax.optimization_barrier(v.astype(jnp.bfloat16)).astype(jnp.float32)

@jax.custom_vjp
def low_back(v):
    return v

def low_keep(v):
    return (low(v), None)

def low_pass(kept, grad):
    return (grad,)

def back_keep(v):
    return (v, None)

def back_low(kept, grad):
    return (low(grad),)
low.defvjp(low_keep, low_pass)
low_back.defvjp(back_keep, back_low)
EPS = 1e-06
HIGH = lax.Precision.HIGHEST

def rms_scale(values):
    return lax.rsqrt(lax.optimization_barrier(jnp.mean(values * values, axis=-1, keepdims=True)) + EPS)

def seq_tables(stream, seq_lens):
    ends = jnp.cumsum(seq_lens)
    after = (stream[:, None] >= ends[None, :]).astype(jnp.int32)
    seq_id = lax.optimization_barrier(jnp.sum(after, axis=1)).astype(jnp.int32)
    position = stream - lax.optimization_barrier(jnp.sum(after * seq_lens[None, :], axis=1))
    return (seq_id, position)

def rotate(values, position):
    half = values.shape[-1] // 2
    freq = 10000.0 ** (-2.0 * jnp.arange(half, dtype=jnp.float32) / values.shape[-1])
    angle = position.astype(jnp.float32)[:, None] * freq[None, :]
    cosine = jnp.cos(angle)[:, None, :]
    sine = jnp.sin(angle)[:, None, :]
    first = values[..., :half]
    second = values[..., half:]
    return jnp.concatenate([first * cosine - second * sine, second * cosine + first * sine], axis=-1)

def route_slots(route_block):
    expert_ids = route_block.reshape(-1)
    hits = (expert_ids[:, None] == jnp.arange(EXPERTS)[None, :]).astype(jnp.int32)
    before = jnp.cumsum(hits, axis=0) - hits
    return (expert_ids, lax.optimization_barrier(jnp.sum(before * hits, axis=1)).astype(jnp.int32))

def group_forward(params, input_group, route_group, stream, seq_lens):
    w_qkv, w_out, w_router, g_attn, g_moe, g_q, g_k, w_gate, w_up, w_down = params
    q_width = HEADS * HD
    kv_width = KV_HEADS * HD
    group_size = HEADS // KV_HEADS
    seq_id, position = seq_tables(stream, seq_lens)
    attn_in = low(input_group * rms_scale(input_group) * g_attn)
    projected = low_back(jnp.dot(attn_in, w_qkv, precision=HIGH))
    query_raw = projected[:, :q_width].reshape(G, HEADS, HD)
    key_raw = projected[:, q_width:q_width + kv_width].reshape(G, KV_HEADS, HD)
    values = low(projected[:, q_width + kv_width:].reshape(G, KV_HEADS, HD))
    queries = low(rotate(query_raw * rms_scale(query_raw) * g_q, position))
    keys = low(rotate(key_raw * rms_scale(key_raw) * g_k, position))
    query_group = queries.reshape(G, KV_HEADS, group_size, HD)
    scores = low_back(jnp.einsum('qhgd,khd->hgqk', query_group, keys, precision=HIGH) * HD ** (-0.5))
    same_seq = seq_id[:, None] == seq_id[None, :]
    scores = jnp.where(same_seq[None, None], scores, -1e+30)
    probs = low(jax.nn.softmax(scores, axis=-1))
    attended = jnp.einsum('hgqk,khd->qhgd', probs, values, precision=HIGH).reshape(G, q_width)
    attended = low_back(low(attended))
    mid = input_group + low_back(jnp.dot(attended, w_out, precision=HIGH))
    moe_in = low(mid * rms_scale(mid) * g_moe)
    logits = low_back(jnp.dot(moe_in, w_router, precision=HIGH))
    chosen_hot = (route_group[:, :, None] == jnp.arange(EXPERTS)[None, None, :]).astype(jnp.float32)
    gate_probs = jax.nn.softmax(lax.optimization_barrier(jnp.sum(chosen_hot * logits[:, None, :], axis=-1)), axis=-1)
    expert_ids, slot_index = jax.vmap(route_slots)(route_group.reshape(N_SHARD, TPD, TOP))
    source = jnp.broadcast_to(jnp.arange(N_SHARD)[:, None], expert_ids.shape)
    token_index = jnp.arange(G * TOP) // TOP
    row_values = moe_in[token_index].reshape(N_SHARD, TPD * TOP, D)
    dispatch = jnp.zeros((EXPERTS, N_SHARD, CAP, D), jnp.float32).at[expert_ids, source, slot_index].set(row_values)
    dispatch = low_back(dispatch)
    gate_part = low_back(jnp.einsum('escd,edf->escf', dispatch, w_gate, precision=HIGH))
    up_part = low_back(jnp.einsum('escd,edf->escf', dispatch, w_up, precision=HIGH))
    hidden = low(jax.nn.silu(gate_part) * up_part)
    expert_out = low_back(low(jnp.einsum('escf,efd->escd', hidden, w_down, precision=HIGH)))
    picked = expert_out[expert_ids, source, slot_index].reshape(G, TOP, D)
    return mid + lax.optimization_barrier(jnp.sum(gate_probs[:, :, None] * picked, axis=1))

def reference(block_input, cotangent, routes, lengths, stream_slot, w_qkv, w_out, w_router, g_attn, g_moe, g_q, g_k, w_gate, w_up, w_down):
    params = tuple((weight.astype(jnp.float32) for weight in (w_qkv, w_out, w_router, g_attn, g_moe, g_q, g_k, w_gate, w_up, w_down)))
    route_groups = routes.reshape(N_REP, N_SHARD, MICRO, TPD, TOP).transpose(0, 2, 1, 3, 4).reshape(N_REP * MICRO, G, TOP)
    streams = stream_slot.reshape(N_REP * MICRO, G)
    seq_lens = lengths.reshape(N_REP * MICRO, SEQS)

    def forward(input_full, weights):
        grouped = input_full.reshape(N_REP, N_SHARD, MICRO, TPD, D).transpose(0, 2, 1, 3, 4).reshape(N_REP * MICRO, G, D)
        step_fn = jax.checkpoint(group_forward)

        def scan_step(carry, items):
            return (carry, step_fn(weights, items[0], items[1], items[2], items[3]))
        _, results = lax.scan(scan_step, jnp.zeros((), jnp.float32), (grouped, route_groups, streams, seq_lens))
        return results.reshape(N_REP, MICRO, N_SHARD, TPD, D).transpose(0, 2, 1, 3, 4).reshape(TOKENS, D)
    mixed, pullback = jax.vjp(forward, block_input.astype(jnp.float32), params)
    grad_input, grads = pullback(cotangent.astype(jnp.float32))
    return (mixed.astype(jnp.bfloat16), grad_input.astype(jnp.bfloat16), grads[0], grads[1], grads[2], grads[3], grads[4], grads[5], grads[6], grads[7], grads[8], grads[9])
```

```python
import functools

import jax
import jax.numpy as jnp
from jax import lax
from jax.experimental import pallas as pl
from jax.experimental.pallas import tpu as pltpu
from jax.sharding import PartitionSpec as P

D = 1024
HEADS = 16
KV_HEADS = 8
HD = 64
HALF = HD // 2
FF = 512
TOP = 8
MICRO = 2
SEQS = 8
SHARDS = 16
REPS = 8
CHIPS = 8
TPD = 128
G = SHARDS * TPD
EXPERTS = 32
LOCAL_EXPERTS = EXPERTS // SHARDS
SLOTS = 48
ROWS = SHARDS * SLOTS
PART = 4
PARTS = SHARDS // PART
CHUNK = 256
CHUNKS = G // CHUNK
HEAD_COLS = 3 * HD
PACK = 256
APART = 256.0
EPS = 1e-06

F32 = jnp.float32
BF16 = jnp.bfloat16
MIB = 1 << 20

BRIEF = pl.CostEstimate(flops=1_000_000, bytes_accessed=1_000_000, transcendentals=0)

SAME_CORE = [[core + 2 * chip for chip in range(CHIPS)] for core in range(2)]
OTHER_CORE = [(index, index ^ 1) for index in range(SHARDS)]


def mm(a, b, left, right):
    return lax.dot_general(a, b, (((left,), (right,)), ((), ())), preferred_element_type=F32)


def rms_scale(values, axis=-1):
    return lax.rsqrt(jnp.mean(values * values, axis=axis, keepdims=True) + EPS)


def norm_back(grad_hat, normed, scale, axis=-1):
    return scale * (grad_hat - normed * jnp.mean(grad_hat * normed, axis=axis, keepdims=True))


def turn(values, cosine, sine):
    first, second = values[:HALF], values[HALF:]
    return jnp.concatenate(
        [first * cosine - second * sine, second * cosine + first * sine], axis=0
    )


def attn_fwd_kernel(
    x_ref,
    w_ref,
    ga_ref,
    gq_ref,
    gk_ref,
    tab_ref,
    ain_ref,
    raw_ref,
    key_ref,
    keyt_ref,
    val_ref,
    query_ref,
    out_ref,
    outf_ref,
    inv_ref,
    valt,
):
    step = pl.program_id(1)
    x = x_ref[...].reshape(CHUNK, D).astype(F32)
    attn_in = (x * rms_scale(x) * ga_ref[...]).astype(BF16)
    ain_ref[0] = attn_in
    raw = mm(w_ref[...], attn_in, 1, 1)
    raw_ref[0, step] = raw[: 2 * HD]
    table = tab_ref[0, step]
    cosine, sine = table[:HALF], table[HALF:HD]
    far, own = table[HD : HD + SEQS], table[HD + SEQS :]
    query_raw, key_raw, value = raw[:HD], raw[HD : 2 * HD], raw[2 * HD :]
    query = turn(query_raw * rms_scale(query_raw, 0) * gq_ref[...], cosine, sine).astype(BF16)
    key = turn(key_raw * rms_scale(key_raw, 0) * gk_ref[...], cosine, sine).astype(BF16)
    pad = jnp.zeros((HD - SEQS, CHUNK), F32)
    query_ref[0, step] = jnp.concatenate(
        [query.astype(F32) * HD**-0.5, far, pad], axis=0
    ).astype(BF16)
    keyt_ref[0, step] = key
    key_rows = jnp.concatenate([key.astype(F32), own, pad], axis=0)
    key_ref[0, pl.ds(step * CHUNK, CHUNK), :] = key_rows.T.astype(BF16)
    place = lax.broadcasted_iota(jnp.int32, (HD, CHUNK), 0)
    val_rows = jnp.concatenate([value, (place < 2).astype(F32)], axis=0)
    val_ref[0, pl.ds(step * CHUNK, CHUNK), :] = val_rows.T.astype(BF16)
    valt[:, pl.ds(pl.multiple_of(step * CHUNK, CHUNK), CHUNK)] = val_rows[: HD + 16].astype(BF16)

    @pl.when(step == CHUNKS - 1)
    def attend():
        tokens = pl.ds(pl.multiple_of(pl.program_id(0) * TPD, TPD), TPD)

        def one(j, carry):
            weights = jnp.exp(mm(key_ref[0], query_ref[0, j], 1, 0)).astype(BF16)
            total = mm(valt[...], weights, 1, 0)
            inv = 1.0 / total[HD : HD + 1]
            attended = total[:HD] * inv
            inv_ref[0, j] = inv
            outf_ref[0, j] = attended
            low = attended.astype(BF16)
            out_ref[2 * j, :, tokens] = low[:, :TPD]
            out_ref[2 * j + 1, :, tokens] = low[:, TPD:]
            return carry

        lax.fori_loop(0, CHUNKS, one, 0)


def attn_fwd(x_all, w_head, attn_gain, query_gain, key_gain, tables):
    whole = lambda *shape: pl.BlockSpec(shape, lambda m, i: (0,) * len(shape))
    each = lambda *shape: pl.BlockSpec((1, *shape), lambda m, i: (m,) + (0,) * len(shape))
    shapes = (
        ((MICRO, G, D), BF16),
        ((MICRO, CHUNKS, 2 * HD, CHUNK), F32),
        ((MICRO, G, 2 * HD), BF16),
        ((MICRO, CHUNKS, HD, CHUNK), BF16),
        ((MICRO, G, 2 * HD), BF16),
        ((MICRO, CHUNKS, 2 * HD, CHUNK), BF16),
        ((SHARDS, HD, MICRO * TPD), BF16),
        ((MICRO, CHUNKS, HD, CHUNK), F32),
        ((MICRO, CHUNKS, 1, CHUNK), F32),
    )
    return pl.pallas_call(
        attn_fwd_kernel,
        grid=(MICRO, CHUNKS),
        in_specs=[
            pl.BlockSpec((CHUNK // TPD, TPD, D), lambda m, i: (i, m, 0)),
            whole(HEAD_COLS, D),
            whole(1, D),
            whole(HD, 1),
            whole(HD, 1),
            each(CHUNKS, HD + 2 * SEQS, CHUNK),
        ],
        out_specs=[
            pl.BlockSpec((1, CHUNK, D), lambda m, i: (m, i, 0)),
        ]
        + [each(*shape[1:]) for shape, _ in shapes[1:6]]
        + [whole(*shapes[6][0])]
        + [each(*shape[1:]) for shape, _ in shapes[7:]],
        out_shape=[jax.ShapeDtypeStruct(shape, dtype) for shape, dtype in shapes],
        scratch_shapes=[pltpu.VMEM((HD + 16, G), BF16)],
        compiler_params=pltpu.CompilerParams(vmem_limit_bytes=60 * MIB),
        cost_estimate=BRIEF,
        name="attn_fwd",
    )(x_all, w_head, attn_gain, query_gain, key_gain, tables)


def attn_bwd_kernel(
    grad_ref,
    outf_ref,
    inv_ref,
    key_ref,
    keyt_ref,
    val_ref,
    query_ref,
    raw_ref,
    ain_ref,
    gq_ref,
    gk_ref,
    tab_ref,
    dproj_ref,
    gw_ref,
    gain_ref,
    dq_s,
    dk_s,
    dv_s,
):
    keyt = jnp.concatenate([keyt_ref[0, j] for j in range(CHUNKS)], axis=1)
    dk_s[...] = jnp.zeros_like(dk_s)
    dv_s[...] = jnp.zeros_like(dv_s)
    pad = jnp.zeros((HD - 2, CHUNK), F32)

    def one(j, carry):
        grad = jnp.concatenate([grad_ref[2 * j], grad_ref[2 * j + 1]], axis=1).astype(F32)
        grad = grad * inv_ref[0, j]
        low = grad.astype(BF16)
        dot = -jnp.sum(low.astype(F32) * outf_ref[0, j], axis=0, keepdims=True)
        dot_high = dot.astype(BF16).astype(F32)
        rows = jnp.concatenate([grad, dot_high, dot - dot_high, pad], axis=0)
        query = query_ref[0, j]
        weights = jnp.exp(mm(key_ref[0], query, 1, 0))
        centred = mm(val_ref[0], rows.astype(BF16), 1, 0)
        dscores = (weights * centred).astype(BF16)
        dq_s[j] = mm(keyt, dscores, 1, 0) * HD**-0.5
        dk_s[...] += mm(dscores, query.astype(F32).T.astype(BF16), 1, 0)
        dv_s[...] += mm(weights.astype(BF16), rows.T.astype(BF16), 1, 0)
        return carry

    lax.fori_loop(0, CHUNKS, one, 0)
    gq, gk = gq_ref[...], gk_ref[...]
    gw_ref[...] = jnp.zeros_like(gw_ref)
    gain_ref[...] = jnp.zeros_like(gain_ref)

    def back(j, carry):
        tokens = pl.ds(j * CHUNK, CHUNK)
        cosine, sine = tab_ref[0, j, :HALF], -tab_ref[0, j, HALF:HD]
        raw = raw_ref[0, j]
        dk = dk_s[tokens, :].T[:HD]
        dv = dv_s[tokens, :].T[:HD]
        parts = []
        gains = []
        for grad, values, gain in ((dq_s[j], raw[:HD], gq), (dk, raw[HD:], gk)):
            normed_grad = turn(grad, cosine, sine)
            scale = rms_scale(values, 0)
            hat = values * scale
            gains.append(jnp.sum(normed_grad * hat, axis=1, keepdims=True))
            parts.append(norm_back(normed_grad * gain, hat, scale, 0))
        dproj = jnp.concatenate(parts + [dv], axis=0).astype(BF16)
        dproj_ref[2 * j] = dproj[:, :TPD]
        dproj_ref[2 * j + 1] = dproj[:, TPD:]
        gw_ref[...] += mm(dproj, ain_ref[0, tokens, :], 1, 0)
        gain_ref[...] += jnp.concatenate(
            [jnp.broadcast_to(g, (HD, TPD)) for g in gains], axis=0
        )
        return carry

    lax.fori_loop(0, CHUNKS, back, 0)


def attn_bwd(m, grad, *operands):
    shapes = (
        ((SHARDS, HEAD_COLS, TPD), BF16),
        ((HEAD_COLS, D), F32),
        ((2 * HD, TPD), F32),
    )
    whole = lambda *shape: pl.BlockSpec(shape, lambda i: (0,) * len(shape))
    each = lambda *shape: pl.BlockSpec((1, *shape), lambda i: (m,) + (0,) * len(shape))
    return pl.pallas_call(
        attn_bwd_kernel,
        grid=(1,),
        in_specs=[whole(*grad.shape)]
        + [each(*v.shape[1:]) if v.shape[0] == MICRO else whole(*v.shape) for v in operands],
        out_specs=[whole(*shape) for shape, _ in shapes],
        out_shape=[jax.ShapeDtypeStruct(shape, dtype) for shape, dtype in shapes],
        scratch_shapes=[
            pltpu.VMEM((CHUNKS, HD, CHUNK), F32),
            pltpu.VMEM((G, 2 * HD), F32),
            pltpu.VMEM((G, 2 * HD), F32),
        ],
        compiler_params=pltpu.CompilerParams(vmem_limit_bytes=60 * MIB),
        cost_estimate=BRIEF,
        name="attn_bwd",
    )(grad, *operands)


def expert_kernel(core_ref, *refs, later, kinds, waits):
    refs = refs[waits:]
    rows_refs, refs = refs[: kinds[0]], refs[kinds[0] :]
    grads_refs, refs = refs[: kinds[1]], refs[kinds[1] :]
    slot_ref, gate_ref, wg_ref, wu_ref, wd_ref, *refs = refs
    before_refs = (None,) * 3
    if later:
        before_refs = (refs[2], refs[0], refs[1])
        refs = refs[3:]
    out_refs, back_refs = refs[:2], refs[2:4]
    route_ref, gg_ref, gu_ref, gd_ref = refs[4:8]
    xs, cs, ps, ys, ds = refs[8:]
    step = pl.program_id(0)
    slots = lax.broadcasted_iota(jnp.int32, (SLOTS, TPD), 0).astype(F32)

    def block(refs, k):
        if len(refs) == 2:
            return refs[k % 2][k // 2]
        return refs[0][k ^ core_ref[0]]

    def hot_of(expert, source):
        return slots == slot_ref[expert, pl.ds(source, 1), :]

    @pl.when(step < PARTS)
    def pick():
        for k in range(PART):
            source = step * PART + k
            hots = [hot_of(e, source) for e in range(LOCAL_EXPERTS)]
            low = jnp.concatenate(hots, axis=0).astype(BF16)
            shape = (LOCAL_EXPERTS, SLOTS, D)
            xs[:, source] = mm(low, block(rows_refs, k), 1, 0).astype(BF16).reshape(shape)
            cs[:, source] = mm(low, block(grads_refs, k), 1, 0).astype(BF16).reshape(shape)
            for e in range(LOCAL_EXPERTS):
                gate = jnp.where(hots[e], gate_ref[e, pl.ds(source, 1), :], 0.0)
                ps[e, source] = jnp.broadcast_to(
                    jnp.sum(gate, axis=1, keepdims=True), (SLOTS, TPD)
                )

    @pl.when((step >= PARTS) & (step < PARTS + LOCAL_EXPERTS))
    def work():
        expert = step - PARTS
        w_gate, w_up, w_down = wg_ref[0], wu_ref[0], wd_ref[0]
        x = xs[expert].reshape(ROWS, D)
        c = cs[expert].reshape(ROWS, D).astype(F32)
        prob = ps[expert].reshape(ROWS, TPD)[:, :1]
        gate = mm(x, w_gate, 1, 0)
        up = mm(x, w_up, 1, 0)
        sigmoid = 1.0 / (1.0 + jnp.exp(-gate))
        active = gate * sigmoid
        hidden = (active * up).astype(BF16)
        made = mm(hidden, w_down, 1, 0).astype(BF16).astype(F32)
        ys[:, expert] = (made * prob).astype(BF16).reshape(SHARDS, SLOTS, D)
        ps[expert] = jnp.broadcast_to(
            jnp.sum(made * c, axis=1, keepdims=True), (ROWS, TPD)
        ).reshape(SHARDS, SLOTS, TPD)
        dmade = (prob * c).astype(BF16)
        dhidden = mm(dmade, w_down, 1, 1)
        dgate = (dhidden * up * (sigmoid + active * (1.0 - sigmoid))).astype(BF16)
        dup = (dhidden * active).astype(BF16)
        drows = mm(dgate, w_gate, 1, 1) + mm(dup, w_up, 1, 1)
        ds[:, expert] = drows.astype(BF16).reshape(SHARDS, SLOTS, D)
        for total_ref, before, left, right in zip(
            (gd_ref, gg_ref, gu_ref), before_refs, (hidden, x, x), (dmade, dgate, dup)
        ):
            term = mm(left, right, 0, 0)
            if later:
                term = term + before[0].astype(F32)
            total_ref[0] = term.astype(BF16)

    @pl.when(step >= PARTS + LOCAL_EXPERTS)
    def put():
        for k in range(PART):
            source = (step - PARTS - LOCAL_EXPERTS) * PART + k
            hots = [hot_of(e, source) for e in range(LOCAL_EXPERTS)]
            low = jnp.concatenate(hots, axis=0).astype(BF16)
            back_refs[k % 2][k // 2] = mm(low, ds[source].reshape(-1, D), 0, 0).astype(BF16)
            out_refs[k % 2][k // 2] = mm(low, ys[source].reshape(-1, D), 0, 0).astype(BF16)
            for e in range(LOCAL_EXPERTS):
                route_ref[e, pl.ds(source, 1), :] = jnp.sum(
                    jnp.where(hots[e], ps[e, source], 0.0), axis=0, keepdims=True
                )


def experts_step(waits, m, core, rows, grads, slot, gate, w_gate, w_up, w_down, previous):
    later = previous is not None
    whole = lambda *shape: pl.BlockSpec(shape, lambda i, at: (0,) * len(shape))
    first = lambda i, at: (jnp.minimum(i, PARTS - 1), 0, 0)
    kinds = (len(rows), 1)
    of_micro = lambda i, at: (jnp.minimum(i, PARTS - 1), m, 0)
    last = lambda i, at: (jnp.maximum(i - PARTS - LOCAL_EXPERTS, 0), 0, 0)
    each = lambda *shape: pl.BlockSpec(
        (1, *shape), lambda i, at: (jnp.clip(i - PARTS, 0, LOCAL_EXPERTS - 1), 0, 0)
    )
    weight_specs = [each(D, FF), each(D, FF), each(FF, D)]
    shapes = [
        *[((CHIPS, TPD, D), BF16)] * 4,
        ((LOCAL_EXPERTS, SHARDS, TPD), F32),
        (w_gate.shape, BF16),
        (w_up.shape, BF16),
        (w_down.shape, BF16),
    ]
    return pl.pallas_call(
        functools.partial(expert_kernel, later=later, kinds=kinds, waits=len(waits)),
        grid_spec=pltpu.PrefetchScalarGridSpec(
            num_scalar_prefetch=1,
            grid=(2 * PARTS + LOCAL_EXPERTS,),
            in_specs=[
                *[pl.BlockSpec(memory_space=pl.ANY)] * len(waits),
                *[pl.BlockSpec((PART // len(rows), TPD, D), first)] * len(rows),
                pl.BlockSpec((PART, TPD, D), of_micro),
            whole(LOCAL_EXPERTS, SHARDS, TPD),
            whole(LOCAL_EXPERTS, SHARDS, TPD),
        ]
        + weight_specs
        + (weight_specs if later else []),
        out_specs=[
            *[pl.BlockSpec((PART // 2, TPD, D), last)] * 4,
            whole(LOCAL_EXPERTS, SHARDS, TPD),
        ]
        + weight_specs,
        scratch_shapes=[
            pltpu.VMEM((LOCAL_EXPERTS, SHARDS, SLOTS, D), BF16),
            pltpu.VMEM((LOCAL_EXPERTS, SHARDS, SLOTS, D), BF16),
            pltpu.VMEM((LOCAL_EXPERTS, SHARDS, SLOTS, TPD), F32),
            pltpu.VMEM((SHARDS, LOCAL_EXPERTS, SLOTS, D), BF16),
            pltpu.VMEM((SHARDS, LOCAL_EXPERTS, SLOTS, D), BF16),
        ],
        ),
        out_shape=[jax.ShapeDtypeStruct(shape, dtype) for shape, dtype in shapes],
        compiler_params=pltpu.CompilerParams(vmem_limit_bytes=60 * MIB),
        cost_estimate=BRIEF,
        name="experts",
    )(core, *waits, *rows, grads, slot, gate, w_gate, w_up, w_down, *(previous if later else ()))


def gather(values):
    return lax.all_gather(values, "shard", axis=0)


def nothing(values_ref, earlier_ref, out_ref):
    del values_ref, earlier_ref, out_ref


def after(values, earlier):
    anywhere = pl.BlockSpec(memory_space=pl.ANY)
    return pl.pallas_call(
        nothing,
        in_specs=[anywhere] * 2,
        out_specs=anywhere,
        out_shape=jax.ShapeDtypeStruct(values.shape, values.dtype),
        input_output_aliases={0: 0},
        cost_estimate=BRIEF,
        name="after",
    )(values, earlier)


Y_SWAP = [(index, (index + 8) % SHARDS) for index in range(SHARDS)]
X_SHIFTS = [
    [(index, index // 8 * 8 + (index + 2 * shift) % 8) for index in range(SHARDS)]
    for shift in range(1, 4)
]


def permute(values, pairs):
    return lax.ppermute(values, "shard", pairs)


def gather_cores(values):
    like = exchange(
        jnp.broadcast_to(values[None], (CHIPS, *values.shape)), groups=SAME_CORE
    )
    return like, permute(like, OTHER_CORE)


def exchange(values, axis="shard", groups=None):
    return lax.all_to_all(
        values, axis, split_axis=0, concat_axis=0, tiled=True, axis_index_groups=groups
    )


def sum_cores(keep, give):
    return (keep.astype(F32) + permute(give, OTHER_CORE).astype(F32)).astype(BF16)


def sum_by_permutes(keep, give, shard):
    x, y = shard % 8 // 2, shard // 8
    chip = sum_cores(keep, give).reshape(2, 4, *keep.shape[1:])
    column = lambda k: lax.dynamic_index_in_dim(chip, (x + k) % 4, 1, keepdims=False)
    total = column(0).astype(F32)
    for k, shift in enumerate(X_SHIFTS):
        total = total + permute(column(k + 1), shift).astype(F32)
    row = lambda k: lax.dynamic_index_in_dim(total, k, 0, keepdims=False)
    return row(y) + permute(row(1 - y).astype(BF16), Y_SWAP).astype(F32)


def routed_softmax(logits, hits):
    top = jnp.max(jnp.where(hits, logits, -jnp.inf), axis=0, keepdims=True)
    powers = jnp.where(hits, jnp.exp(jnp.where(hits, logits - top, 0.0)), 0.0)
    return powers / jnp.sum(powers, axis=0, keepdims=True)


def local(
    block_input,
    cotangent,
    routes,
    lengths,
    stream_slot,
    w_qkv,
    w_out,
    w_router,
    g_attn,
    g_moe,
    g_q,
    g_k,
    w_gate,
    w_up,
    w_down,
):
    shard = lax.axis_index("shard")
    core = shard % 2
    q_width = HEADS * HD
    kv_width = KV_HEADS * HD
    own_rows = D // SHARDS
    micro = lambda values, m: values[m * TPD : (m + 1) * TPD]

    x_all = gather(block_input)

    doubled = lambda part: jnp.repeat(part.reshape(own_rows, KV_HEADS, HD), 2, axis=1)
    column = lambda v: jnp.pad(v, (0, own_rows - v.shape[0]))[:, None]
    small = jnp.concatenate([w_router, column(g_attn), column(g_moe), column(g_q), column(g_k)], 1)
    small = jnp.pad(small, ((0, 0), (0, PACK - HEAD_COLS - small.shape[1])))
    packed = jnp.concatenate(
        [
            w_qkv[:, :q_width].reshape(own_rows, HEADS, HD),
            doubled(w_qkv[:, q_width : q_width + kv_width]),
            doubled(w_qkv[:, q_width + kv_width :]),
            jnp.broadcast_to(small[:, None], (own_rows, SHARDS, PACK - HEAD_COLS)),
        ],
        axis=2,
    )
    packed = exchange(packed.transpose(1, 0, 2))
    flat = packed.reshape(D, PACK)
    w_head = flat[:, :HEAD_COLS].T
    rest = flat[:, HEAD_COLS:].astype(F32)
    router = flat[:, HEAD_COLS : HEAD_COLS + EXPERTS]
    attn_gain = rest[:, EXPERTS][None]
    moe_gain = rest[:, EXPERTS + 1][None]
    quarter = rest.reshape(SHARDS, own_rows, -1)[:, : HD // SHARDS]
    query_gain = quarter[:, :, EXPERTS + 2].reshape(HD, 1)
    key_gain = quarter[:, :, EXPERTS + 3].reshape(HD, 1)

    freq = 10000.0 ** (-2.0 * jnp.arange(HALF, dtype=F32) / HD)
    earlier = jnp.triu(jnp.ones((TPD, TPD), BF16), 1)

    hits = []
    for m in range(MICRO):
        named = micro(routes, m).T
        hits.append(jnp.any(named[None] == jnp.arange(EXPERTS)[:, None, None], axis=1))
    extra = jnp.stack(hits).astype(BF16).reshape(MICRO * 4, D)
    extra = jnp.pad(extra, ((0, 16 - MICRO * 4), (0, 0)))
    ordered = jnp.arange(SHARDS) ^ core
    ends = jnp.cumsum(lengths[0], axis=1)
    stream = stream_slot[0][:, None, :]
    past = (stream >= ends[:, :, None]).astype(jnp.int32)
    seq_id = jnp.sum(past, axis=1, keepdims=True)
    position = stream - jnp.sum(past * lengths[0][:, :, None], axis=1, keepdims=True)
    angle = freq[:, None] * position.astype(F32)
    own = (seq_id == jnp.arange(SEQS)[:, None]).astype(F32)
    tables = jnp.concatenate([jnp.cos(angle), jnp.sin(angle), (own - 1.0) * APART, own], axis=1)
    tables = tables.reshape(MICRO, -1, CHUNKS, CHUNK).transpose(0, 2, 1, 3)
    for ready in (flat, tables):
        x_all = after(x_all, ready)
    grads_all = gather(after(jnp.concatenate([cotangent, extra, w_out], axis=0), x_all))
    hits_all = grads_all[:, MICRO * TPD : MICRO * TPD + 16]
    hits_all = hits_all.reshape(SHARDS, 2 * MICRO, EXPERTS, TPD)[ordered]
    out_full = grads_all[:, MICRO * TPD + 16 :].reshape(q_width, D)
    attn_in_all, raw, key, keyt, val, query, out, outf, inv = attn_fwd(
        x_all, w_head, attn_gain, query_gain, key_gain, tables
    )
    attended = after(exchange(out), grads_all).reshape(q_width, MICRO * TPD)
    x = block_input.astype(F32)
    mid = x + mm(attended, out_full, 0, 0)
    moe_scale = rms_scale(mid)
    moe_hat = mid * moe_scale
    moe_in = (moe_hat * moe_gain).astype(BF16)
    rows_all = [gather_cores(micro(moe_in, 0)), (gather(micro(moe_in, 1)),)]

    experts_own = shard * LOCAL_EXPERTS
    grads, sums, chips = None, [], []
    for m in range(MICRO):
        hit = hits_all[:, m]
        before = jnp.einsum("set,tu->seu", hit, earlier, preferred_element_type=F32)
        slot = jnp.where(hit > 0, before, -1.0)
        slot = lax.dynamic_slice_in_dim(slot, experts_own, LOCAL_EXPERTS, 1).transpose(1, 0, 2)
        if m == 1:
            logits = mm(router, rows_all[1][0].reshape(G, D), 0, 1)
            logits = logits.reshape(EXPERTS, SHARDS, TPD)[:, ordered].reshape(EXPERTS, G)
        else:
            logits = jnp.stack(
                [mm(router, rows.reshape(G // 2, D), 0, 1) for rows in rows_all[m]], axis=1
            ).reshape(EXPERTS, 2, CHIPS, TPD)
            logits = logits.transpose(0, 2, 1, 3).reshape(EXPERTS, G)
        gate = routed_softmax(logits, hit.transpose(1, 0, 2).reshape(EXPERTS, G) > 0)
        gate = lax.dynamic_slice_in_dim(gate, experts_own, LOCAL_EXPERTS, 0)
        *parts, route, g_gate, g_up, g_down = experts_step(
            (chips[0],) if m else (),
            m,
            core.reshape(1),
            rows_all[m],
            grads_all,
            slot,
            gate.reshape(LOCAL_EXPERTS, SHARDS, TPD),
            w_gate,
            w_up,
            w_down,
            grads,
        )
        grads = (g_gate, g_up, g_down)
        sums.append((parts[:2], route))
        if m == 0:
            chips.append(sum_cores(*parts[2:]))
            qkv_full = lax.all_gather(after(w_qkv, route), "shard", axis=0, tiled=True)
    grad_experts = lax.psum(tuple(grads), "rep")

    out_part = jnp.zeros((q_width, D), F32)
    small_part = jnp.zeros((D, EXPERTS + 1), F32)
    grad_mid, grad_attended, back_attn = [], [], []
    for m in range(MICRO):
        route = sums[m][1]
        scale, hat, rows_in = (micro(v, m) for v in (moe_scale, moe_hat, moe_in))
        route_grad = exchange(route.transpose(1, 0, 2)[ordered]).reshape(EXPERTS, TPD)
        came = exchange(chips[m], groups=SAME_CORE)
        if m:
            came = after(came, back_attn[0][0])
        dmoe_in = jnp.sum(came.astype(F32), axis=0)
        gate = routed_softmax(mm(router, rows_in, 0, 1), hits[m])
        dlogits = gate * (route_grad - jnp.sum(gate * route_grad, axis=0, keepdims=True))
        dlogits = dlogits.astype(BF16)
        dmoe_in = dmoe_in + mm(dlogits, router, 0, 1)
        moe_part = jnp.sum(dmoe_in * hat, axis=0)
        small_part = small_part + jnp.concatenate(
            [mm(rows_in, dlogits, 0, 1), moe_part[:, None]], axis=1
        )
        dmid = micro(cotangent, m).astype(F32) + norm_back(dmoe_in * moe_gain, hat, scale)
        low = dmid.astype(BF16)
        out_part = out_part + mm(attended[:, m * TPD : (m + 1) * TPD], low, 1, 0)
        dattended = mm(out_full, low, 1, 1).astype(BF16)
        grad_mid.append(dmid)
        grad_attended.append(exchange(dattended.reshape(SHARDS, HD, TPD)))
        if m == 0:
            chips.append(sum_cores(after(parts[2], grad_attended[0]), parts[3]))
            grad_attended[0] = after(grad_attended[0], chips[1])
        back_attn.append(
            attn_bwd(
                m,
                grad_attended[m],
                outf,
                inv,
                key,
                keyt,
                val,
                query,
                raw,
                attn_in_all,
                query_gain,
                key_gain,
                tables,
            )
        )
    blocks = out_part.astype(BF16).reshape(CHIPS, 2, own_rows, D)
    out_own = sum_by_permutes(
        lax.dynamic_index_in_dim(blocks, core, 1, keepdims=False),
        lax.dynamic_index_in_dim(blocks, 1 - core, 1, keepdims=False),
        shard,
    )

    outputs = []
    for m in range(MICRO):
        keep, give = sums[m][0]
        total = sum_by_permutes(keep, after(give, grad_attended[1]), shard)
        outputs.append((micro(mid, m) + total).astype(BF16))

    input_grads = []
    attn_part = jnp.zeros((D,), F32)
    head_part = jnp.zeros((HEAD_COLS, D), F32)
    gain_part = jnp.zeros((2 * HD,), F32)
    for m in range(MICRO):
        dproj, head_grad, gains = back_attn[m]
        head_part = head_part + head_grad
        gain_part = gain_part + gains[:, 0]
        dproj = exchange(dproj if m else after(dproj, grad_attended[1]))
        paired = dproj[:, HD:].astype(F32).reshape(KV_HEADS, 2, 2, HD, TPD).sum(axis=1)
        dproj = jnp.concatenate(
            [
                dproj[:, :HD].reshape(q_width, TPD),
                paired[:, 0].reshape(kv_width, TPD).astype(BF16),
                paired[:, 1].reshape(kv_width, TPD).astype(BF16),
            ],
            axis=0,
        )
        here = micro(x, m)
        scale = rms_scale(here)
        hat = here * scale
        dattn_in = mm(dproj, qkv_full, 0, 1)
        attn_part = attn_part + jnp.sum(dattn_in * hat, axis=0)
        dx = grad_mid[m] + norm_back(dattn_in * attn_gain, hat, scale)
        input_grads.append(dx.astype(BF16))

    fours = gain_part.reshape(2, SHARDS, HD // SHARDS).transpose(1, 2, 0)
    fours = jnp.pad(fours, ((0, 0), (0, own_rows - HD // SHARDS), (0, 0))).reshape(D, 2)
    packed = jnp.concatenate([head_part.T, small_part, attn_part[:, None], fours], axis=1)
    packed = jnp.pad(packed, ((0, 0), (0, PACK - packed.shape[1]))).astype(BF16)
    for output in outputs:
        packed = after(packed, output)
    got = exchange(packed.reshape(SHARDS, own_rows, PACK)).astype(F32)
    flat = lambda part: part.transpose(1, 0, 2).reshape(own_rows, -1)
    pair_sum = lambda part: flat(part.reshape(KV_HEADS, 2, own_rows, HD).sum(axis=1))
    owned = jnp.concatenate(
        [
            flat(got[:, :, :HD]),
            pair_sum(got[:, :, HD : 2 * HD]),
            pair_sum(got[:, :, 2 * HD : HEAD_COLS]),
            out_own.astype(F32),
            got[:, :, HEAD_COLS:].sum(axis=0),
            jnp.zeros((own_rows, HD), F32),
        ],
        axis=1,
    ).astype(BF16)
    width = owned.shape[1]
    share = jnp.sum(
        exchange(owned.reshape(REPS, own_rows // REPS, width), "rep").astype(F32), axis=0
    ).astype(BF16)
    owned = exchange(jnp.broadcast_to(share[None], (REPS, *share.shape)), "rep")
    owned = owned.reshape(own_rows, width).astype(F32)
    base = q_width + 2 * kv_width + D
    four = HD // SHARDS
    return (
        jnp.concatenate(outputs, axis=0),
        jnp.concatenate(input_grads, axis=0),
        owned[:, : base - D],
        owned[:, base - D : base],
        owned[:, base : base + EXPERTS],
        owned[:, base + EXPERTS + 1],
        owned[:, base + EXPERTS],
        owned[:four, base + EXPERTS + 2],
        owned[:four, base + EXPERTS + 3],
        *(g.astype(F32) for g in grad_experts),
    )


def solution(mesh):
    rows = P(("rep", "shard"), None)
    rep, split, vector = P("rep", None, None), P("shard", None), P("shard")
    expert = P("shard", None, None)
    return jax.shard_map(
        local,
        mesh=mesh,
        in_specs=(rows,) * 3 + (rep,) * 2 + (split,) * 3 + (vector,) * 4 + (expert,) * 3,
        out_specs=(rows,) * 2 + (split,) * 3 + (vector,) * 4 + (expert,) * 3,
        check_vma=False,
    )
```

```python
import functools

import jax
import jax.numpy as jnp
from jax import lax
from jax.experimental import pallas as pl
from jax.experimental.pallas import tpu as pltpu
from jax.sharding import PartitionSpec as P

D = 1024
HEADS = 16
KV_HEADS = 8
HD = 64
HALF = HD // 2
FF = 512
TOP = 8
MICRO = 2
SEQS = 8
SHARDS = 16
REPS = 8
CHIPS = 8
TPD = 128
G = SHARDS * TPD
EXPERTS = 32
LOCAL_EXPERTS = EXPERTS // SHARDS
SLOTS = 48
ROWS = SHARDS * SLOTS
PART = 4
PARTS = SHARDS // PART
TALL = TPD + 16
CHUNK = 256
CHUNKS = G // CHUNK
HEAD_COLS = 3 * HD
PACK = 256
APART = 256.0
EPS = 1e-06

F32 = jnp.float32
BF16 = jnp.bfloat16
MIB = 1 << 20

BRIEF = pl.CostEstimate(flops=1_000_000, bytes_accessed=1_000_000, transcendentals=0)

SAME_CORE = [[core + 2 * chip for chip in range(CHIPS)] for core in range(2)]
OTHER_CORE = [(index, index ^ 1) for index in range(SHARDS)]


def mm(a, b, left, right):
    return lax.dot_general(a, b, (((left,), (right,)), ((), ())), preferred_element_type=F32)


def rms_scale(values, axis=-1):
    return lax.rsqrt(jnp.mean(values * values, axis=axis, keepdims=True) + EPS)


def norm_back(grad_hat, normed, scale, axis=-1):
    return scale * (grad_hat - normed * jnp.mean(grad_hat * normed, axis=axis, keepdims=True))


def turn(values, cosine, sine):
    first, second = values[:HALF], values[HALF:]
    return jnp.concatenate(
        [first * cosine - second * sine, second * cosine + first * sine], axis=0
    )


def attn_fwd_kernel(
    x_ref,
    w_ref,
    ga_ref,
    gq_ref,
    gk_ref,
    tab_ref,
    ain_ref,
    raw_ref,
    key_ref,
    keyt_ref,
    val_ref,
    query_ref,
    out_ref,
    outf_ref,
    inv_ref,
    valt,
):
    step = pl.program_id(1)
    x = x_ref[...].reshape(CHUNK, D).astype(F32)
    attn_in = (x * rms_scale(x) * ga_ref[...]).astype(BF16)
    ain_ref[0] = attn_in
    raw = mm(w_ref[...], attn_in, 1, 1)
    raw_ref[0, step] = raw[: 2 * HD]
    table = tab_ref[0, step]
    cosine, sine = table[:HALF], table[HALF:HD]
    far, own = table[HD : HD + SEQS], table[HD + SEQS :]
    query_raw, key_raw, value = raw[:HD], raw[HD : 2 * HD], raw[2 * HD :]
    query = turn(query_raw * rms_scale(query_raw, 0) * gq_ref[...], cosine, sine).astype(BF16)
    key = turn(key_raw * rms_scale(key_raw, 0) * gk_ref[...], cosine, sine).astype(BF16)
    pad = jnp.zeros((HD - SEQS, CHUNK), F32)
    query_ref[0, step] = jnp.concatenate(
        [query.astype(F32) * HD**-0.5, far, pad], axis=0
    ).astype(BF16)
    keyt_ref[0, step] = key
    key_rows = jnp.concatenate([key.astype(F32), own, pad], axis=0)
    key_ref[0, pl.ds(step * CHUNK, CHUNK), :] = key_rows.T.astype(BF16)
    place = lax.broadcasted_iota(jnp.int32, (HD, CHUNK), 0)
    val_rows = jnp.concatenate([value, (place < 2).astype(F32)], axis=0)
    val_ref[0, pl.ds(step * CHUNK, CHUNK), :] = val_rows.T.astype(BF16)
    valt[:, pl.ds(pl.multiple_of(step * CHUNK, CHUNK), CHUNK)] = val_rows[: HD + 16].astype(BF16)

    @pl.when(step == CHUNKS - 1)
    def attend():
        tokens = pl.ds(pl.multiple_of(pl.program_id(0) * TPD, TPD), TPD)

        def one(j, carry):
            weights = jnp.exp(mm(key_ref[0], query_ref[0, j], 1, 0)).astype(BF16)
            total = mm(valt[...], weights, 1, 0)
            inv = 1.0 / total[HD : HD + 1]
            attended = total[:HD] * inv
            inv_ref[0, j] = inv
            outf_ref[0, j] = attended
            low = attended.astype(BF16)
            out_ref[2 * j, :, tokens] = low[:, :TPD]
            out_ref[2 * j + 1, :, tokens] = low[:, TPD:]
            return carry

        lax.fori_loop(0, CHUNKS, one, 0)


def attn_fwd(x_all, w_head, attn_gain, query_gain, key_gain, tables):
    whole = lambda *shape: pl.BlockSpec(shape, lambda m, i: (0,) * len(shape))
    each = lambda *shape: pl.BlockSpec((1, *shape), lambda m, i: (m,) + (0,) * len(shape))
    shapes = (
        ((MICRO, G, D), BF16),
        ((MICRO, CHUNKS, 2 * HD, CHUNK), F32),
        ((MICRO, G, 2 * HD), BF16),
        ((MICRO, CHUNKS, HD, CHUNK), BF16),
        ((MICRO, G, 2 * HD), BF16),
        ((MICRO, CHUNKS, 2 * HD, CHUNK), BF16),
        ((SHARDS, HD, MICRO * TPD), BF16),
        ((MICRO, CHUNKS, HD, CHUNK), F32),
        ((MICRO, CHUNKS, 1, CHUNK), F32),
    )
    return pl.pallas_call(
        attn_fwd_kernel,
        grid=(MICRO, CHUNKS),
        in_specs=[
            pl.BlockSpec((CHUNK // TPD, TPD, D), lambda m, i: (i, m, 0)),
            whole(HEAD_COLS, D),
            whole(1, D),
            whole(HD, 1),
            whole(HD, 1),
            each(CHUNKS, HD + 2 * SEQS, CHUNK),
        ],
        out_specs=[
            pl.BlockSpec((1, CHUNK, D), lambda m, i: (m, i, 0)),
        ]
        + [each(*shape[1:]) for shape, _ in shapes[1:6]]
        + [whole(*shapes[6][0])]
        + [each(*shape[1:]) for shape, _ in shapes[7:]],
        out_shape=[jax.ShapeDtypeStruct(shape, dtype) for shape, dtype in shapes],
        scratch_shapes=[pltpu.VMEM((HD + 16, G), BF16)],
        compiler_params=pltpu.CompilerParams(vmem_limit_bytes=60 * MIB),
        cost_estimate=BRIEF,
        name="attn_fwd",
    )(x_all, w_head, attn_gain, query_gain, key_gain, tables)


def attn_bwd_kernel(
    grad_ref,
    outf_ref,
    inv_ref,
    key_ref,
    keyt_ref,
    val_ref,
    query_ref,
    raw_ref,
    ain_ref,
    gq_ref,
    gk_ref,
    tab_ref,
    dproj_ref,
    gw_ref,
    gain_ref,
    dq_s,
    dk_s,
    dv_s,
):
    keyt = jnp.concatenate([keyt_ref[0, j] for j in range(CHUNKS)], axis=1)
    dk_s[...] = jnp.zeros_like(dk_s)
    dv_s[...] = jnp.zeros_like(dv_s)
    pad = jnp.zeros((HD - 2, CHUNK), F32)

    def one(j, carry):
        grad = jnp.concatenate([grad_ref[2 * j], grad_ref[2 * j + 1]], axis=1).astype(F32)
        grad = grad * inv_ref[0, j]
        low = grad.astype(BF16)
        dot = -jnp.sum(low.astype(F32) * outf_ref[0, j], axis=0, keepdims=True)
        dot_high = dot.astype(BF16).astype(F32)
        rows = jnp.concatenate([grad, dot_high, dot - dot_high, pad], axis=0)
        query = query_ref[0, j]
        weights = jnp.exp(mm(key_ref[0], query, 1, 0))
        centred = mm(val_ref[0], rows.astype(BF16), 1, 0)
        dscores = (weights * centred).astype(BF16)
        dq_s[j] = mm(keyt, dscores, 1, 0) * HD**-0.5
        dk_s[...] += mm(dscores, query.astype(F32).T.astype(BF16), 1, 0)
        dv_s[...] += mm(weights.astype(BF16), rows.T.astype(BF16), 1, 0)
        return carry

    lax.fori_loop(0, CHUNKS, one, 0)
    gq, gk = gq_ref[...], gk_ref[...]
    gw_ref[...] = jnp.zeros_like(gw_ref)
    gain_ref[...] = jnp.zeros_like(gain_ref)

    def back(j, carry):
        tokens = pl.ds(j * CHUNK, CHUNK)
        cosine, sine = tab_ref[0, j, :HALF], -tab_ref[0, j, HALF:HD]
        raw = raw_ref[0, j]
        dk = dk_s[tokens, :].T[:HD]
        dv = dv_s[tokens, :].T[:HD]
        parts = []
        gains = []
        for grad, values, gain in ((dq_s[j], raw[:HD], gq), (dk, raw[HD:], gk)):
            normed_grad = turn(grad, cosine, sine)
            scale = rms_scale(values, 0)
            hat = values * scale
            gains.append(jnp.sum(normed_grad * hat, axis=1, keepdims=True))
            parts.append(norm_back(normed_grad * gain, hat, scale, 0))
        dproj = jnp.concatenate(parts + [dv], axis=0).astype(BF16)
        dproj_ref[2 * j] = dproj[:, :TPD]
        dproj_ref[2 * j + 1] = dproj[:, TPD:]
        gw_ref[...] += mm(dproj, ain_ref[0, tokens, :], 1, 0)
        gain_ref[...] += jnp.concatenate(
            [jnp.broadcast_to(g, (HD, TPD)) for g in gains], axis=0
        )
        return carry

    lax.fori_loop(0, CHUNKS, back, 0)


def attn_bwd(m, grad, *operands):
    shapes = (
        ((SHARDS, HEAD_COLS, TPD), BF16),
        ((HEAD_COLS, D), F32),
        ((2 * HD, TPD), F32),
    )
    whole = lambda *shape: pl.BlockSpec(shape, lambda i: (0,) * len(shape))
    each = lambda *shape: pl.BlockSpec((1, *shape), lambda i: (m,) + (0,) * len(shape))
    return pl.pallas_call(
        attn_bwd_kernel,
        grid=(1,),
        in_specs=[whole(*grad.shape)]
        + [each(*v.shape[1:]) if v.shape[0] == MICRO else whole(*v.shape) for v in operands],
        out_specs=[whole(*shape) for shape, _ in shapes],
        out_shape=[jax.ShapeDtypeStruct(shape, dtype) for shape, dtype in shapes],
        scratch_shapes=[
            pltpu.VMEM((CHUNKS, HD, CHUNK), F32),
            pltpu.VMEM((G, 2 * HD), F32),
            pltpu.VMEM((G, 2 * HD), F32),
        ],
        compiler_params=pltpu.CompilerParams(vmem_limit_bytes=60 * MIB),
        cost_estimate=BRIEF,
        name="attn_bwd",
    )(grad, *operands)


def routed_softmax(logits, hits):
    top = jnp.max(jnp.where(hits, logits, -jnp.inf), axis=0, keepdims=True)
    powers = jnp.where(hits, jnp.exp(jnp.where(hits, logits - top, 0.0)), 0.0)
    return powers / jnp.sum(powers, axis=0, keepdims=True)


def expert_kernel(core_ref, *refs, later, kinds, waits):
    refs = refs[waits:]
    rows_refs, refs = refs[: kinds[0]], refs[kinds[0] :]
    grads_refs, refs = refs[: kinds[1]], refs[kinds[1] :]
    slot_ref, hit_ref, router_ref, wg_ref, wu_ref, wd_ref, *refs = refs
    before_refs = (None,) * 3
    if later:
        before_refs = (refs[2], refs[0], refs[1])
        refs = refs[3:]
    out_refs, back_refs = refs[:2], refs[2:4]
    gg_ref, gu_ref, gd_ref = refs[4:7]
    xs, cs, ps, ys, ds = refs[7:]
    step = pl.program_id(0)
    slots = lax.broadcasted_iota(jnp.int32, (SLOTS, TPD), 0).astype(F32)

    def block(refs, k):
        if len(refs) == 2:
            return refs[k % 2][k // 2]
        return refs[0][k ^ core_ref[0]]

    def hot_of(expert, source):
        return slots == slot_ref[expert, pl.ds(source, 1), :]

    @pl.when(step < PARTS)
    def pick():
        for k in range(PART):
            source = step * PART + k
            hots = [hot_of(e, source) for e in range(LOCAL_EXPERTS)]
            low = jnp.concatenate(hots, axis=0).astype(BF16)
            shape = (LOCAL_EXPERTS, SLOTS, D)
            rows = block(rows_refs, k)
            xs[:, source] = mm(low, rows, 1, 0).astype(BF16).reshape(shape)
            cs[:, source] = mm(low, block(grads_refs, k), 1, 0).astype(BF16).reshape(shape)
            gates = routed_softmax(mm(router_ref[...], rows, 1, 1), hit_ref[source] > 0)
            named = lax.broadcasted_iota(jnp.int32, (EXPERTS, TPD), 0) - core_ref[1]
            for e in range(LOCAL_EXPERTS):
                gate = jnp.sum(jnp.where(named == e, gates, 0.0), axis=0, keepdims=True)
                gate = jnp.where(hots[e], gate, 0.0)
                ps[e, source] = jnp.broadcast_to(
                    jnp.sum(gate, axis=1, keepdims=True), (SLOTS, TPD)
                )

    @pl.when((step >= PARTS) & (step < PARTS + LOCAL_EXPERTS))
    def work():
        expert = step - PARTS
        w_gate, w_up, w_down = wg_ref[0], wu_ref[0], wd_ref[0]
        x = xs[expert].reshape(ROWS, D)
        c = cs[expert].reshape(ROWS, D).astype(F32)
        prob = ps[expert].reshape(ROWS, TPD)[:, :1]
        gate = mm(x, w_gate, 1, 0)
        up = mm(x, w_up, 1, 0)
        sigmoid = 1.0 / (1.0 + jnp.exp(-gate))
        active = gate * sigmoid
        hidden = (active * up).astype(BF16)
        made = mm(hidden, w_down, 1, 0).astype(BF16).astype(F32)
        ys[:, expert] = (made * prob).astype(BF16).reshape(SHARDS, SLOTS, D)
        ps[expert] = jnp.broadcast_to(
            jnp.sum(made * c, axis=1, keepdims=True), (ROWS, TPD)
        ).reshape(SHARDS, SLOTS, TPD)
        dmade = (prob * c).astype(BF16)
        dhidden = mm(dmade, w_down, 1, 1)
        dgate = (dhidden * up * (sigmoid + active * (1.0 - sigmoid))).astype(BF16)
        dup = (dhidden * active).astype(BF16)
        drows = mm(dgate, w_gate, 1, 1) + mm(dup, w_up, 1, 1)
        ds[:, expert] = drows.astype(BF16).reshape(SHARDS, SLOTS, D)
        for total_ref, before, left, right in zip(
            (gd_ref, gg_ref, gu_ref), before_refs, (hidden, x, x), (dmade, dgate, dup)
        ):
            term = mm(left, right, 0, 0)
            if later:
                term = term + before[0].astype(F32)
            total_ref[0] = term.astype(BF16)

    @pl.when(step >= PARTS + LOCAL_EXPERTS)
    def put():
        for k in range(PART):
            source = (step - PARTS - LOCAL_EXPERTS) * PART + k
            hots = [hot_of(e, source) for e in range(LOCAL_EXPERTS)]
            low = jnp.concatenate(hots, axis=0).astype(BF16)
            back_refs[k % 2][k // 2, :TPD] = mm(low, ds[source].reshape(-1, D), 0, 0).astype(BF16)
            out_refs[k % 2][k // 2] = mm(low, ys[source].reshape(-1, D), 0, 0).astype(BF16)
            pieces = []
            for e in range(LOCAL_EXPERTS):
                route = jnp.where(hots[e], ps[e, source], 0.0)
                route = jnp.sum(route, axis=0, keepdims=True)
                high = route.astype(BF16).astype(F32)
                pieces += [high, route - high]
            lanes = jnp.concatenate(pieces, axis=1)
            row = jnp.concatenate(
                [jnp.where(core_ref[0] == c, lanes, 0.0) for c in range(2)], axis=1
            )
            place = lax.broadcasted_iota(jnp.int32, (TALL - TPD, D), 0)
            back_refs[k % 2][k // 2, TPD:] = jnp.where(place == 0, row, 0.0).astype(BF16)


def experts_step(waits, core, rows, grads, slot, hit, router, w_gate, w_up, w_down, previous):
    later = previous is not None
    whole = lambda *shape: pl.BlockSpec(shape, lambda i, at: (0,) * len(shape))
    first = lambda i, at: (jnp.minimum(i, PARTS - 1), 0, 0)
    kinds = (len(rows), 1)
    second = lambda i, at: (jnp.minimum(i, PARTS - 1), 1 if later else 0, 0)
    last = lambda i, at: (jnp.maximum(i - PARTS - LOCAL_EXPERTS, 0), 0, 0)
    each = lambda *shape: pl.BlockSpec(
        (1, *shape), lambda i, at: (jnp.clip(i - PARTS, 0, LOCAL_EXPERTS - 1), 0, 0)
    )
    weight_specs = [each(D, FF), each(D, FF), each(FF, D)]
    shapes = [
        *[((CHIPS, TPD, D), BF16)] * 2,
        *[((CHIPS, TALL, D), BF16)] * 2,
        (w_gate.shape, BF16),
        (w_up.shape, BF16),
        (w_down.shape, BF16),
    ]
    return pl.pallas_call(
        functools.partial(expert_kernel, later=later, kinds=kinds, waits=len(waits)),
        grid_spec=pltpu.PrefetchScalarGridSpec(
            num_scalar_prefetch=1,
            grid=(2 * PARTS + LOCAL_EXPERTS,),
            in_specs=[
                *[pl.BlockSpec(memory_space=pl.ANY)] * len(waits),
                *[pl.BlockSpec((PART // len(rows), TPD, D), first)] * len(rows),
                pl.BlockSpec((PART, TPD, D), second),
            whole(LOCAL_EXPERTS, SHARDS, TPD),
            whole(SHARDS, EXPERTS, TPD),
            whole(EXPERTS, D),
        ]
        + weight_specs
        + (weight_specs if later else []),
        out_specs=[
            *[pl.BlockSpec((PART // 2, TPD, D), last)] * 2,
            *[pl.BlockSpec((PART // 2, TALL, D), last)] * 2,
        ]
        + weight_specs,
        scratch_shapes=[
            pltpu.VMEM((LOCAL_EXPERTS, SHARDS, SLOTS, D), BF16),
            pltpu.VMEM((LOCAL_EXPERTS, SHARDS, SLOTS, D), BF16),
            pltpu.VMEM((LOCAL_EXPERTS, SHARDS, SLOTS, TPD), F32),
            pltpu.VMEM((SHARDS, LOCAL_EXPERTS, SLOTS, D), BF16),
            pltpu.VMEM((SHARDS, LOCAL_EXPERTS, SLOTS, D), BF16),
        ],
        ),
        out_shape=[jax.ShapeDtypeStruct(shape, dtype) for shape, dtype in shapes],
        compiler_params=pltpu.CompilerParams(vmem_limit_bytes=60 * MIB),
        cost_estimate=BRIEF,
        name="experts",
    )(core, *waits, *rows, grads, slot, hit, router, w_gate, w_up, w_down, *(previous if later else ()))


def gather(values):
    return lax.all_gather(values, "shard", axis=0)


def nothing(values_ref, earlier_ref, out_ref):
    del values_ref, earlier_ref, out_ref


def after(values, earlier):
    anywhere = pl.BlockSpec(memory_space=pl.ANY)
    return pl.pallas_call(
        nothing,
        in_specs=[anywhere] * 2,
        out_specs=anywhere,
        out_shape=jax.ShapeDtypeStruct(values.shape, values.dtype),
        input_output_aliases={0: 0},
        cost_estimate=BRIEF,
        name="after",
    )(values, earlier)


Y_SWAP = [(index, (index + 8) % SHARDS) for index in range(SHARDS)]
X_SHIFTS = [
    [(index, index // 8 * 8 + (index + 2 * shift) % 8) for index in range(SHARDS)]
    for shift in range(1, 4)
]


def permute(values, pairs):
    return lax.ppermute(values, "shard", pairs)


def exchange(values, axis="shard", groups=None):
    return lax.all_to_all(
        values, axis, split_axis=0, concat_axis=0, tiled=True, axis_index_groups=groups
    )


def call(kernel, name, shapes, *operands, scalars=(), waits=(), specs=None):
    count, held = len(operands), len(scalars)
    specs = dict(specs or {})
    whole = lambda shape: pl.BlockSpec(shape, lambda i, *_: (0,) * len(shape))

    def body(*refs):
        kernel(*refs[: held + count], *refs[held + count + len(waits) :])

    return pl.pallas_call(
        body,
        grid_spec=pltpu.PrefetchScalarGridSpec(
            num_scalar_prefetch=held,
            grid=(1,),
            in_specs=[specs.get(i, whole(v.shape)) for i, v in enumerate(operands)]
            + [pl.BlockSpec(memory_space=pl.ANY)] * len(waits),
            out_specs=[whole(shape) for shape, _ in shapes],
        ),
        out_shape=[jax.ShapeDtypeStruct(shape, dtype) for shape, dtype in shapes],
        compiler_params=pltpu.CompilerParams(vmem_limit_bytes=60 * MIB),
        cost_estimate=BRIEF,
        name=name,
    )(*scalars, *operands, *waits)


def block(shape, *index):
    return pl.BlockSpec(shape, lambda i, *_: index)


OUT_ROWS = block((SHARDS, D // SHARDS, D), 0, 2, 0)


def mid_kernel(att_ref, wout_ref, x_ref, gain_ref, cot_ref, wqkv_ref, mid_ref, first_ref, second_ref):
    mid = x_ref[...].astype(F32) + mm(att_ref[...], wout_ref[...].reshape(HEADS * HD, D), 0, 0)
    mid_ref[...] = mid
    moe_in = (mid * rms_scale(mid) * gain_ref[...]).astype(BF16)
    first_ref[...] = jnp.broadcast_to(moe_in[None, :TPD], (CHIPS, TPD, D))
    own = D // SHARDS
    second_ref[:TPD] = moe_in[TPD:]
    second_ref[TPD : 2 * TPD] = cot_ref[TPD:]
    second_ref[2 * TPD : 2 * TPD + own] = wqkv_ref[:, :D]
    second_ref[2 * TPD + own :] = wqkv_ref[:, D:]


def add_kernel(x_ref, *refs, pairs):
    step = pl.program_id(0)
    del x_ref
    total = [
        (refs[2 * i][...].astype(F32) + refs[2 * i + 1][...].astype(F32)).astype(BF16)
        for i in range(pairs)
    ]
    out_refs = refs[2 * pairs :]
    if len(out_refs) == 1:
        out_refs[0][...] = total[0]
        return
    for k, out_ref in enumerate(out_refs):

        @pl.when(step == k)
        def put(out_ref=out_ref):
            for i in range(pairs):
                out_ref[i] = total[i][:, 0]


def sum_cores(keep, give):
    parts = 4
    spec = pl.BlockSpec((CHIPS // parts, *keep.shape[1:]), lambda i, at: (i, 0, 0))
    return pl.pallas_call(
        functools.partial(add_kernel, pairs=1),
        grid_spec=pltpu.PrefetchScalarGridSpec(
            num_scalar_prefetch=1, grid=(parts,), in_specs=[spec] * 2, out_specs=[spec]
        ),
        out_shape=[jax.ShapeDtypeStruct(keep.shape, BF16)],
        cost_estimate=BRIEF,
        name="sum_cores",
    )(jnp.zeros((1,), jnp.int32), keep, permute(give, OTHER_CORE))[0]


def sum_cores_by_x(pairs, shard):
    own = pairs[0][0].shape[1:]
    spec = pl.BlockSpec((2, 1, *own), lambda i, at: (0, (at[0] + i) % 4, 0, 0))
    shape = (len(pairs), 2, *own)
    whole = pl.BlockSpec(shape, lambda i, at: (0,) * len(shape))
    operands = []
    for keep, give in pairs:
        operands += [keep.reshape(2, 4, *own), permute(give, OTHER_CORE).reshape(2, 4, *own)]
    return pl.pallas_call(
        functools.partial(add_kernel, pairs=len(pairs)),
        grid_spec=pltpu.PrefetchScalarGridSpec(
            num_scalar_prefetch=1,
            grid=(4,),
            in_specs=[spec] * len(operands),
            out_specs=[whole] * 4,
        ),
        out_shape=[jax.ShapeDtypeStruct(shape, BF16)] * 4,
        compiler_params=pltpu.CompilerParams(vmem_limit_bytes=60 * MIB),
        cost_estimate=BRIEF,
        name="sum_cores_by_x",
    )((shard % 8 // 2).reshape(1), *operands)


def along_x_kernel(y_ref, a_ref, b_ref, c_ref, d_ref, keep_ref, give_ref):
    total = sum(ref[...].astype(F32) for ref in (a_ref, b_ref, c_ref, d_ref))
    own = y_ref[0] == 0
    keep_ref[...] = jnp.where(own, total[:, 0], total[:, 1])
    give_ref[...] = jnp.where(own, total[:, 1], total[:, 0]).astype(BF16)


def send_along_x(columns, wait):
    came = [permute(after(c, wait), shift) for c, shift in zip(columns[1:], X_SHIFTS)]
    return [columns[0], *came]


def sum_along_x(came, shard, wait):
    shape = (came[0].shape[0], *came[0].shape[2:])
    return call(
        along_x_kernel,
        "sum_along_x",
        [(shape, F32), (shape, BF16)],
        *came,
        scalars=[(shard // 8).reshape(1)],
        waits=(wait,),
    )


def sum_along_y(keep, give):
    return keep + permute(give, Y_SWAP).astype(F32)


def expert_end_kernel(
    came_ref,
    mid_ref,
    cot_ref,
    router_ref,
    gain_ref,
    hit_ref,
    wout_ref,
    dmid_ref,
    low_ref,
    datt_ref,
    small_ref,
):
    dmoe_in = sum(came_ref[chip, :TPD].astype(F32) for chip in range(CHIPS))
    rows = []
    for chip in range(CHIPS):
        lanes = came_ref[chip, TPD:].astype(F32)[:1]
        for k in range(4):
            rows.append(
                lanes[:, 2 * k * TPD : (2 * k + 1) * TPD]
                + lanes[:, (2 * k + 1) * TPD : (2 * k + 2) * TPD]
            )
    route_grad = jnp.concatenate(rows, axis=0)
    mid = mid_ref[...]
    scale = rms_scale(mid)
    hat = mid * scale
    gain = gain_ref[...]
    rows_in = (hat * gain).astype(BF16)
    router = router_ref[...]
    gate = routed_softmax(mm(router, rows_in, 1, 1), hit_ref[...] > 0)
    dlogits = gate * (route_grad - jnp.sum(gate * route_grad, axis=0, keepdims=True))
    dlogits = dlogits.astype(BF16)
    dmoe_in = dmoe_in + mm(dlogits, router, 0, 0)
    small_ref[:EXPERTS] = mm(dlogits, rows_in, 1, 0)
    small_ref[EXPERTS:] = jnp.broadcast_to(
        jnp.sum(dmoe_in * hat, axis=0, keepdims=True), (8, D)
    )
    dmid = cot_ref[...].astype(F32) + norm_back(dmoe_in * gain, hat, scale)
    dmid_ref[...] = dmid
    low = dmid.astype(BF16)
    low_ref[...] = low
    datt = mm(wout_ref[...].reshape(HEADS * HD, D), low, 1, 1)
    datt_ref[...] = datt.astype(BF16).reshape(SHARDS, HD, TPD)


def out_kernel(core_ref, att_ref, first_ref, second_ref, keep_ref, give_ref):
    att = att_ref[...]
    total = mm(att[:, :TPD], first_ref[...], 1, 0) + mm(att[:, TPD:], second_ref[...], 1, 0)
    total = total.astype(BF16).reshape(CHIPS, 2, D // SHARDS, D)
    for core in range(2):

        @pl.when(core_ref[0] == core)
        def put(core=core):
            keep_ref[...] = total[:, core]
            give_ref[...] = total[:, 1 - core]


def input_kernel(dproj_ref, left_ref, right_ref, x_ref, dmid_ref, gain_ref, out_ref):
    queries = dproj_ref[:, :HD, :].reshape(HEADS * HD, TPD)
    paired = dproj_ref[:, HD:, :].astype(F32).reshape(KV_HEADS, 2, 2 * HD, TPD)
    paired = (paired[:, 0] + paired[:, 1]).astype(BF16)
    both = [paired[:, :HD].reshape(KV_HEADS * HD, TPD), paired[:, HD:].reshape(KV_HEADS * HD, TPD)]
    grad = mm(left_ref[...].reshape(D, D), queries, 1, 0)
    grad = grad + mm(right_ref[...].reshape(D, D), jnp.concatenate(both, axis=0), 1, 0)
    x = x_ref[...].astype(F32)
    scale = rms_scale(x)
    grad = norm_back(grad.T * gain_ref[...], x * scale, scale)
    out_ref[...] = (dmid_ref[...] + grad).astype(BF16)


def pack_kernel(ha_ref, hb_ref, sa_ref, sb_ref, ga_ref, gb_ref, out_ref):
    small = sa_ref[...] + sb_ref[...]
    gains = ga_ref[...] + gb_ref[...]
    lane = lax.broadcasted_iota(jnp.int32, (HD, D), 1)
    place = lax.broadcasted_iota(jnp.int32, (HD, D), 0)
    four = HD // SHARDS
    there = lane == place // four * (D // SHARDS) + place % four
    rows = [
        jnp.sum(jnp.where(there, gain[:, :1], 0.0), axis=0, keepdims=True)
        for gain in (gains[:HD], gains[HD:])
    ]
    rows = jnp.concatenate(
        [
            ha_ref[...] + hb_ref[...],
            small[: EXPERTS + 1],
            *rows,
            jnp.zeros((PACK - HEAD_COLS - EXPERTS - 3, D), F32),
        ],
        axis=0,
    )
    out_ref[...] = rows.T.astype(BF16).reshape(SHARDS, D // SHARDS, PACK)


def own_kernel(got_ref, keep_ref, came_ref, out_ref):
    left = lax.broadcasted_iota(jnp.int32, (D // SHARDS, TPD), 1) < HD
    swap = lambda v: pltpu.roll(v, HD, 1)
    query_key = [got_ref[h, :, :TPD].astype(F32) for h in range(HEADS)]
    value_rest = [got_ref[h, :, TPD:].astype(F32) for h in range(HEADS)]
    pairs = range(0, HEADS, 2)
    queries = [jnp.where(left, query_key[h], swap(query_key[h + 1])) for h in pairs]
    keys = [query_key[h] + query_key[h + 1] for h in pairs]
    values = [value_rest[h] + value_rest[h + 1] for h in pairs]
    rest = sum(values)
    keys = [jnp.where(left, swap(keys[h]), keys[h + 1]) for h in range(0, KV_HEADS, 2)]
    values = [jnp.where(left, values[h], swap(values[h + 1])) for h in range(0, KV_HEADS, 2)]
    out = keep_ref[...] + came_ref[...].astype(F32)
    out_ref[...] = jnp.concatenate([*queries, *keys, *values, out, rest], axis=1).astype(BF16)


def share_kernel(parts_ref, out_ref):
    total = sum(parts_ref[rep].astype(F32) for rep in range(REPS)).astype(BF16)
    out_ref[...] = jnp.broadcast_to(total[None], out_ref.shape)


def last_kernel(all_ref, wqkv_ref, gain_ref, qkv_ref, out_ref, rest_ref):
    width = wqkv_ref.shape[1]
    rows = all_ref[...].astype(F32).reshape(D // SHARDS, -1)
    qkv_ref[...] = rows[:, :width]
    out_ref[...] = rows[:, width : width + D]
    gain = jnp.sum(rows[:, :width] * wqkv_ref[...].astype(F32), axis=1, keepdims=True)
    left = lax.broadcasted_iota(jnp.int32, (D // SHARDS, TPD), 1) < HD
    rest_ref[...] = jnp.where(left, gain / gain_ref[...], rows[:, width + D :])


def local(
    block_input,
    cotangent,
    routes,
    lengths,
    stream_slot,
    w_qkv,
    w_out,
    w_router,
    g_attn,
    g_moe,
    g_q,
    g_k,
    w_gate,
    w_up,
    w_down,
):
    shard = lax.axis_index("shard")
    core = shard % 2
    q_width = HEADS * HD
    kv_width = KV_HEADS * HD
    own_rows = D // SHARDS
    micro = lambda values, m: values[m * TPD : (m + 1) * TPD]

    x_all = gather(block_input)

    doubled = lambda part: jnp.repeat(part.reshape(own_rows, KV_HEADS, HD), 2, axis=1)
    column = lambda v: jnp.pad(v, (0, own_rows - v.shape[0]))[:, None]
    small = jnp.concatenate([w_router, column(g_attn), column(g_moe), column(g_q), column(g_k)], 1)
    small = jnp.pad(small, ((0, 0), (0, PACK - HEAD_COLS - small.shape[1])))
    packed = jnp.concatenate(
        [
            w_qkv[:, :q_width].reshape(own_rows, HEADS, HD),
            doubled(w_qkv[:, q_width : q_width + kv_width]),
            doubled(w_qkv[:, q_width + kv_width :]),
            jnp.broadcast_to(small[:, None], (own_rows, SHARDS, PACK - HEAD_COLS)),
        ],
        axis=2,
    )
    packed = exchange(packed.transpose(1, 0, 2))
    flat = packed.reshape(D, PACK)
    w_head = flat[:, :HEAD_COLS].T
    rest = flat[:, HEAD_COLS:].astype(F32)
    router = flat[:, HEAD_COLS : HEAD_COLS + EXPERTS]
    attn_gain = rest[:, EXPERTS][None]
    moe_gain = rest[:, EXPERTS + 1][None]
    quarter = rest.reshape(SHARDS, own_rows, -1)[:, : HD // SHARDS]
    query_gain = quarter[:, :, EXPERTS + 2].reshape(HD, 1)
    key_gain = quarter[:, :, EXPERTS + 3].reshape(HD, 1)

    freq = 10000.0 ** (-2.0 * jnp.arange(HALF, dtype=F32) / HD)
    earlier = jnp.triu(jnp.ones((TPD, TPD), BF16), 1)

    hits = []
    for m in range(MICRO):
        named = micro(routes, m).T
        hits.append(jnp.any(named[None] == jnp.arange(EXPERTS)[:, None, None], axis=1))
    extra = jnp.stack(hits).astype(BF16).reshape(MICRO * 4, D)
    extra = jnp.pad(extra, ((0, 16 - MICRO * 4), (0, 0)))
    ordered = jnp.arange(SHARDS) ^ core
    ends = jnp.cumsum(lengths[0], axis=1)
    stream = stream_slot[0][:, None, :]
    past = (stream >= ends[:, :, None]).astype(jnp.int32)
    seq_id = jnp.sum(past, axis=1, keepdims=True)
    position = stream - jnp.sum(past * lengths[0][:, :, None], axis=1, keepdims=True)
    angle = freq[:, None] * position.astype(F32)
    own = (seq_id == jnp.arange(SEQS)[:, None]).astype(F32)
    tables = jnp.concatenate([jnp.cos(angle), jnp.sin(angle), (own - 1.0) * APART, own], axis=1)
    tables = tables.reshape(MICRO, -1, CHUNKS, CHUNK).transpose(0, 2, 1, 3)
    for ready in (flat, tables):
        x_all = after(x_all, ready)
    packet = jnp.concatenate([micro(cotangent, 0), w_out, extra], axis=0)
    packet = gather(after(packet, x_all))
    hits_all = packet[:, TPD + own_rows :].reshape(SHARDS, 2 * MICRO, EXPERTS, TPD)
    hits_all = hits_all[:, :MICRO][ordered].transpose(1, 0, 2, 3)
    before = jnp.einsum("mset,tu->mseu", hits_all, earlier, preferred_element_type=F32)
    slot_all = jnp.where(hits_all > 0, before, -1.0)
    experts_own = shard * LOCAL_EXPERTS
    slot_all = lax.dynamic_slice_in_dim(slot_all, experts_own, LOCAL_EXPERTS, 2)
    slot_all = slot_all.transpose(0, 2, 1, 3)
    attn_in_all, raw, key, keyt, val, query, out, outf, inv = attn_fwd(
        x_all, w_head, attn_gain, query_gain, key_gain, tables
    )
    attended = after(after(exchange(out), packet), slot_all).reshape(q_width, MICRO * TPD)
    mid, rows_first, rows_second = call(
        mid_kernel,
        "mid",
        [((MICRO * TPD, D), F32), ((CHIPS, TPD, D), BF16), ((3 * TPD, D), BF16)],
        attended,
        packet,
        block_input,
        moe_gain,
        cotangent,
        w_qkv,
        specs={1: OUT_ROWS},
    )
    rows_first = exchange(rows_first, groups=SAME_CORE)
    rows_first = (rows_first, permute(rows_first, OTHER_CORE))
    rows_second = gather(rows_second)

    own_experts = jnp.stack([core, experts_own])
    router_rows = router.T
    grads, sums, chips = None, [], []
    for m in range(MICRO):
        *parts, g_gate, g_up, g_down = experts_step(
            (chips[0],) if m else (),
            own_experts,
            (rows_second,) if m else rows_first,
            rows_second if m else packet,
            slot_all[m],
            hits_all[m].astype(F32),
            router_rows,
            w_gate,
            w_up,
            w_down,
            grads,
        )
        grads = (g_gate, g_up, g_down)
        sums.append(parts)
        if m == 0:
            chips.append(sum_cores(*parts[2:]))
            came = exchange(chips[0], groups=SAME_CORE)
    grad_experts = lax.psum(tuple(after(grad, came) for grad in grads), "rep")

    def expert_end(m, came):
        rows = block((TPD, D), m, 0)
        return call(
            expert_end_kernel,
            "expert_end",
            [
                ((TPD, D), F32),
                ((TPD, D), BF16),
                ((SHARDS, HD, TPD), BF16),
                ((EXPERTS + 8, D), F32),
            ],
            came,
            mid,
            cotangent,
            router_rows,
            moe_gain,
            hits[m].astype(F32),
            packet,
            specs={1: rows, 2: rows, 6: OUT_ROWS},
        )

    def attention_back(m, grad):
        return attn_bwd(
            m,
            grad,
            outf,
            inv,
            key,
            keyt,
            val,
            query,
            raw,
            attn_in_all,
            query_gain,
            key_gain,
            tables,
        )

    dmid_first, low_first, dattended, small_first = expert_end(0, came)

    def rest():
        grad_first = exchange(dattended)
        chip = sum_cores(*sums[1][2:])
        outs = sum_cores_by_x([parts[:2] for parts in sums], shard)
        chip = after(chip, grad_first)
        came = exchange(chip, groups=SAME_CORE)
        for ready in (chip, outs[0]):
            grad_first = after(grad_first, ready)
        dproj_first, head_first, gains_first = attention_back(0, grad_first)
        came = after(came, dproj_first)
        dmid_second, low_second, second, small_second = expert_end(1, came)
        second = exchange(second)
        keep, give = call(
            out_kernel,
            "out_part",
            [((CHIPS, own_rows, D), BF16)] * 2,
            attended,
            low_first,
            low_second,
            scalars=[core.reshape(1)],
        )
        out_own = sum_cores_by_x([(keep, give)], shard)
        dproj_first = after(after(dproj_first, second), out_own[0])
        outs = send_along_x(outs, second)
        out_own = send_along_x(out_own, second)
        second = after(second, dproj_first)
        dproj_second, head_second, gains_second = attention_back(1, second)
        dproj_first = exchange(dproj_first)
        outs = sum_along_x(outs, shard, dproj_second)
        keep, give = sum_along_x(out_own, shard, dproj_second)
        (packed,) = call(
            pack_kernel,
            "pack",
            [((SHARDS, own_rows, PACK), BF16)],
            head_first,
            head_second,
            small_first,
            small_second,
            gains_first,
            gains_second,
        )
        dproj_second = exchange(after(dproj_second, dproj_first))
        dproj_all = [dproj_first, dproj_second]
        for ready in (keep, outs[0], dproj_second):
            packed = after(packed, ready)
        packed = exchange(packed)
        output = (mid + sum_along_y(*outs).reshape(mid.shape)).astype(BF16)
        input_grads = []
        for m in range(MICRO):
            rows = block((TPD, D), m, 0)
            input_grads += call(
                input_kernel,
                "input_grad",
                [((TPD, D), BF16)],
                dproj_all[m],
                rows_second,
                rows_second,
                block_input,
                (dmid_first, dmid_second)[m],
                attn_gain,
                specs={
                    1: block((SHARDS, own_rows, D), 0, 4, 0),
                    2: block((SHARDS, own_rows, D), 0, 5, 0),
                    3: rows,
                },
            )
        width = q_width + 2 * kv_width
        (owned,) = call(
            own_kernel,
            "own",
            [((own_rows, width + D + TPD), BF16)],
            packed,
            keep[0],
            permute(give, Y_SWAP)[0],
        )
        owned = exchange(owned.reshape(REPS, own_rows // REPS, -1), "rep")
        (share,) = call(
            share_kernel, "share", [(owned.shape, BF16)], owned, waits=(output,)
        )
        grad_qkv, grad_out, rest = call(
            last_kernel,
            "last",
            [((own_rows, width), F32), ((own_rows, D), F32), ((own_rows, TPD), F32)],
            exchange(share, "rep"),
            w_qkv,
            g_attn.astype(F32)[:, None],
        )
        four = HD // SHARDS
        return (
            output,
            jnp.concatenate(input_grads, axis=0),
            grad_qkv,
            grad_out,
            rest[:, HD : HD + EXPERTS],
            rest[:, 0],
            rest[:, HD + EXPERTS],
            rest[:four, HD + EXPERTS + 1],
            rest[:four, HD + EXPERTS + 2],
        )

    def none():
        return jax.tree.map(lambda v: jnp.zeros(v.shape, v.dtype), jax.eval_shape(rest))

    results = lax.cond(lengths[0, 0, 0] > 0, rest, none)
    return (*results, *(g.astype(F32) for g in grad_experts))


def solution(mesh):
    rows = P(("rep", "shard"), None)
    rep, split, vector = P("rep", None, None), P("shard", None), P("shard")
    expert = P("shard", None, None)
    return jax.shard_map(
        local,
        mesh=mesh,
        in_specs=(rows,) * 3 + (rep,) * 2 + (split,) * 3 + (vector,) * 4 + (expert,) * 3,
        out_specs=(rows,) * 2 + (split,) * 3 + (vector,) * 4 + (expert,) * 3,
        check_vma=False,
    )
```

```python
import functools

import jax
import jax.numpy as jnp
from jax import lax
from jax.experimental import pallas as pl
from jax.experimental.pallas import tpu as pltpu
from jax.sharding import PartitionSpec as P

D = 1024
HEADS = 16
KV_HEADS = 8
HD = 64
HALF = HD // 2
FF = 512
TOP = 8
MICRO = 2
SEQS = 8
SHARDS = 16
REPS = 8
CHIPS = 8
TPD = 128
G = SHARDS * TPD
EXPERTS = 32
LOCAL_EXPERTS = EXPERTS // SHARDS
SLOTS = 48
ROWS = SHARDS * SLOTS
PART = 4
PARTS = SHARDS // PART
TALL = TPD + 16
CHUNK = 256
CHUNKS = G // CHUNK
SPAN = 1024
HEAD_COLS = 3 * HD
PACK = 256
APART = 256.0
EPS = 1e-06

F32 = jnp.float32
BF16 = jnp.bfloat16
MIB = 1 << 20

BRIEF = pl.CostEstimate(flops=1_000_000, bytes_accessed=1_000_000, transcendentals=0)

SAME_CORE = [[core + 2 * chip for chip in range(CHIPS)] for core in range(2)]
OTHER_CORE = [(index, index ^ 1) for index in range(SHARDS)]


def mm(a, b, left, right):
    return lax.dot_general(a, b, (((left,), (right,)), ((), ())), preferred_element_type=F32)


def rms_scale(values, axis=-1):
    return lax.rsqrt(jnp.mean(values * values, axis=axis, keepdims=True) + EPS)


def norm_back(grad_hat, normed, scale, axis=-1):
    return scale * (grad_hat - normed * jnp.mean(grad_hat * normed, axis=axis, keepdims=True))


def turn(values, cosine, sine):
    first, second = values[:HALF], values[HALF:]
    return jnp.concatenate(
        [first * cosine - second * sine, second * cosine + first * sine], axis=0
    )


def attn_fwd_kernel(
    x_ref,
    w_ref,
    ga_ref,
    gq_ref,
    gk_ref,
    tab_ref,
    ain_ref,
    raw_ref,
    key_ref,
    keyt_ref,
    val_ref,
    query_ref,
    out_ref,
    outf_ref,
    inv_ref,
    valt,
):
    step = pl.program_id(1)
    x = x_ref[...].reshape(SPAN, D).astype(F32)
    attn_in = (x * rms_scale(x) * ga_ref[...]).astype(BF16)
    ain_ref[0] = attn_in
    raw_all = mm(attn_in, w_ref[...], 1, 0).T
    pad = jnp.zeros((HD - SEQS, CHUNK), F32)
    place = lax.broadcasted_iota(jnp.int32, (HD, CHUNK), 0)
    for k in range(SPAN // CHUNK):
        chunk = step * (SPAN // CHUNK) + k
        tokens = pl.ds(pl.multiple_of(chunk * CHUNK, CHUNK), CHUNK)
        raw = raw_all[:, k * CHUNK : (k + 1) * CHUNK]
        raw_ref[0, chunk] = raw[: 2 * HD]
        table = tab_ref[0, chunk]
        cosine, sine = table[:HALF], table[HALF:HD]
        far, own = table[HD : HD + SEQS], table[HD + SEQS :]
        query_raw, key_raw, value = raw[:HD], raw[HD : 2 * HD], raw[2 * HD : HEAD_COLS]
        query = turn(query_raw * rms_scale(query_raw, 0) * gq_ref[...], cosine, sine).astype(BF16)
        key = turn(key_raw * rms_scale(key_raw, 0) * gk_ref[...], cosine, sine).astype(BF16)
        query_ref[0, chunk] = jnp.concatenate(
            [query.astype(F32) * HD**-0.5, far, pad], axis=0
        ).astype(BF16)
        keyt_ref[0, chunk] = key
        key_ref[0, tokens, :] = jnp.concatenate([key.astype(F32), own, pad], axis=0).T.astype(BF16)
        val_rows = jnp.concatenate([value, (place < 2).astype(F32)], axis=0)
        val_ref[0, tokens, :] = val_rows.T.astype(BF16)
        valt[:, tokens] = val_rows[: HD + 16].astype(BF16)

    @pl.when(step == G // SPAN - 1)
    def attend():
        tokens = pl.ds(pl.multiple_of(pl.program_id(0) * TPD, TPD), TPD)

        def one(j, carry):
            weights = jnp.exp(mm(key_ref[0], query_ref[0, j], 1, 0)).astype(BF16)
            total = mm(valt[...], weights, 1, 0)
            inv = 1.0 / total[HD : HD + 1]
            attended = total[:HD] * inv
            inv_ref[0, j] = inv
            outf_ref[0, j] = attended
            low = attended.astype(BF16)
            out_ref[2 * j, :, tokens] = low[:, :TPD]
            out_ref[2 * j + 1, :, tokens] = low[:, TPD:]
            return carry

        lax.fori_loop(0, CHUNKS, one, 0, unroll=True)


def attn_fwd(x_all, w_head, attn_gain, query_gain, key_gain, tables):
    whole = lambda *shape: pl.BlockSpec(shape, lambda m, i: (0,) * len(shape))
    each = lambda *shape: pl.BlockSpec((1, *shape), lambda m, i: (m,) + (0,) * len(shape))
    shapes = (
        ((MICRO, G, D), BF16),
        ((MICRO, CHUNKS, 2 * HD, CHUNK), F32),
        ((MICRO, G, 2 * HD), BF16),
        ((MICRO, CHUNKS, HD, CHUNK), BF16),
        ((MICRO, G, 2 * HD), BF16),
        ((MICRO, CHUNKS, 2 * HD, CHUNK), BF16),
        ((SHARDS, HD, MICRO * TPD), BF16),
        ((MICRO, CHUNKS, HD, CHUNK), F32),
        ((MICRO, CHUNKS, 1, CHUNK), F32),
    )
    return pl.pallas_call(
        attn_fwd_kernel,
        grid=(MICRO, G // SPAN),
        in_specs=[
            pl.BlockSpec((SPAN // TPD, TPD, D), lambda m, i: (i, m, 0)),
            whole(D, PACK),
            whole(1, D),
            whole(HD, 1),
            whole(HD, 1),
            each(CHUNKS, HD + 2 * SEQS, CHUNK),
        ],
        out_specs=[
            pl.BlockSpec((1, SPAN, D), lambda m, i: (m, i, 0)),
        ]
        + [each(*shape[1:]) for shape, _ in shapes[1:6]]
        + [whole(*shapes[6][0])]
        + [each(*shape[1:]) for shape, _ in shapes[7:]],
        out_shape=[jax.ShapeDtypeStruct(shape, dtype) for shape, dtype in shapes],
        scratch_shapes=[pltpu.VMEM((HD + 16, G), BF16)],
        compiler_params=pltpu.CompilerParams(vmem_limit_bytes=60 * MIB),
        cost_estimate=BRIEF,
        name="attn_fwd",
    )(x_all, w_head, attn_gain, query_gain, key_gain, tables)


def attn_bwd_kernel(
    grad_ref,
    outf_ref,
    inv_ref,
    key_ref,
    keyt_ref,
    val_ref,
    query_ref,
    raw_ref,
    ain_ref,
    gq_ref,
    gk_ref,
    tab_ref,
    dproj_ref,
    gw_ref,
    gain_ref,
    dq_s,
    dk_s,
    dv_s,
):
    keyt = jnp.concatenate([keyt_ref[0, j] for j in range(CHUNKS)], axis=1)
    dk_s[...] = jnp.zeros_like(dk_s)
    dv_s[...] = jnp.zeros_like(dv_s)
    pad = jnp.zeros((HD - 2, CHUNK), F32)

    def one(j, carry):
        grad = jnp.concatenate([grad_ref[2 * j], grad_ref[2 * j + 1]], axis=1).astype(F32)
        grad = grad * inv_ref[0, j]
        low = grad.astype(BF16)
        dot = -jnp.sum(low.astype(F32) * outf_ref[0, j], axis=0, keepdims=True)
        dot_high = dot.astype(BF16).astype(F32)
        rows = jnp.concatenate([grad, dot_high, dot - dot_high, pad], axis=0)
        query = query_ref[0, j]
        weights = jnp.exp(mm(key_ref[0], query, 1, 0))
        centred = mm(val_ref[0], rows.astype(BF16), 1, 0)
        dscores = (weights * centred).astype(BF16)
        dq_s[j] = mm(keyt, dscores, 1, 0) * HD**-0.5
        dk_s[...] += mm(dscores, query.astype(F32).T.astype(BF16), 1, 0)
        dv_s[...] += mm(weights.astype(BF16), rows.T.astype(BF16), 1, 0)
        return carry

    lax.fori_loop(0, CHUNKS, one, 0, unroll=True)
    gq, gk = gq_ref[...], gk_ref[...]
    gw_ref[...] = jnp.zeros_like(gw_ref)
    gain_ref[...] = jnp.zeros_like(gain_ref)

    def back(j, carry):
        tokens = pl.ds(j * CHUNK, CHUNK)
        cosine, sine = tab_ref[0, j, :HALF], -tab_ref[0, j, HALF:HD]
        raw = raw_ref[0, j]
        dk = dk_s[tokens, :].T[:HD]
        dv = dv_s[tokens, :].T[:HD]
        parts = []
        gains = []
        for grad, values, gain in ((dq_s[j], raw[:HD], gq), (dk, raw[HD:], gk)):
            normed_grad = turn(grad, cosine, sine)
            scale = rms_scale(values, 0)
            hat = values * scale
            gains.append(jnp.sum(normed_grad * hat, axis=1, keepdims=True))
            parts.append(norm_back(normed_grad * gain, hat, scale, 0))
        dproj = jnp.concatenate(parts + [dv], axis=0).astype(BF16)
        dproj_ref[2 * j] = dproj[:, :TPD]
        dproj_ref[2 * j + 1] = dproj[:, TPD:]
        gw_ref[...] += mm(dproj, ain_ref[0, tokens, :], 1, 0)
        gain_ref[...] += jnp.concatenate(
            [jnp.broadcast_to(g, (HD, TPD)) for g in gains], axis=0
        )
        return carry

    lax.fori_loop(0, CHUNKS, back, 0, unroll=2)


def attn_bwd(m, grad, *operands):
    shapes = (
        ((SHARDS, HEAD_COLS, TPD), BF16),
        ((HEAD_COLS, D), F32),
        ((2 * HD, TPD), F32),
    )
    whole = lambda *shape: pl.BlockSpec(shape, lambda i: (0,) * len(shape))
    each = lambda *shape: pl.BlockSpec((1, *shape), lambda i: (m,) + (0,) * len(shape))
    return pl.pallas_call(
        attn_bwd_kernel,
        grid=(1,),
        in_specs=[whole(*grad.shape)]
        + [each(*v.shape[1:]) if v.shape[0] == MICRO else whole(*v.shape) for v in operands],
        out_specs=[whole(*shape) for shape, _ in shapes],
        out_shape=[jax.ShapeDtypeStruct(shape, dtype) for shape, dtype in shapes],
        scratch_shapes=[
            pltpu.VMEM((CHUNKS, HD, CHUNK), F32),
            pltpu.VMEM((G, 2 * HD), F32),
            pltpu.VMEM((G, 2 * HD), F32),
        ],
        compiler_params=pltpu.CompilerParams(vmem_limit_bytes=60 * MIB),
        cost_estimate=BRIEF,
        name="attn_bwd",
    )(grad, *operands)


def routed_softmax(logits, hits):
    top = jnp.max(jnp.where(hits, logits, -jnp.inf), axis=0, keepdims=True)
    powers = jnp.where(hits, jnp.exp(jnp.where(hits, logits - top, 0.0)), 0.0)
    return powers / jnp.sum(powers, axis=0, keepdims=True)


def expert_kernel(core_ref, *refs, later, kinds, waits):
    refs = refs[waits:]
    rows_refs, refs = refs[: kinds[0]], refs[kinds[0] :]
    grads_refs, refs = refs[: kinds[1]], refs[kinds[1] :]
    slot_ref, hit_ref, router_ref, wg_ref, wu_ref, wd_ref, *refs = refs
    before_refs = (None,) * 3
    if later:
        before_refs = (refs[2], refs[0], refs[1])
        refs = refs[3:]
    out_refs, back_refs = refs[:2], refs[2:4]
    gg_ref, gu_ref, gd_ref = refs[4:7]
    xs, cs, ps, ys, ds = refs[7:]
    step = pl.program_id(0)
    slots = lax.broadcasted_iota(jnp.int32, (SLOTS, TPD), 0).astype(F32)

    def block(refs, k):
        if len(refs) == 2:
            return refs[k % 2][k // 2]
        return refs[0][k ^ core_ref[0]]

    def hot_of(expert, source):
        return slots == slot_ref[expert, pl.ds(source, 1), :]

    @pl.when(step < PARTS)
    def pick():
        for k in range(PART):
            source = step * PART + k
            hots = [hot_of(e, source) for e in range(LOCAL_EXPERTS)]
            low = jnp.concatenate(hots, axis=0).astype(BF16)
            shape = (LOCAL_EXPERTS, SLOTS, D)
            rows = block(rows_refs, k)
            xs[:, source] = mm(low, rows, 1, 0).astype(BF16).reshape(shape)
            cs[:, source] = mm(low, block(grads_refs, k), 1, 0).astype(BF16).reshape(shape)
            gates = routed_softmax(mm(router_ref[...], rows, 1, 1), hit_ref[source] > 0)
            named = lax.broadcasted_iota(jnp.int32, (EXPERTS, TPD), 0) - core_ref[1]
            for e in range(LOCAL_EXPERTS):
                gate = jnp.sum(jnp.where(named == e, gates, 0.0), axis=0, keepdims=True)
                gate = jnp.where(hots[e], gate, 0.0)
                ps[e, source] = jnp.broadcast_to(
                    jnp.sum(gate, axis=1, keepdims=True), (SLOTS, TPD)
                )

    @pl.when((step >= PARTS) & (step < PARTS + LOCAL_EXPERTS))
    def work():
        expert = step - PARTS
        w_gate, w_up, w_down = wg_ref[0], wu_ref[0], wd_ref[0]
        x = xs[expert].reshape(ROWS, D)
        c = cs[expert].reshape(ROWS, D).astype(F32)
        prob = ps[expert].reshape(ROWS, TPD)[:, :1]
        gate = mm(x, w_gate, 1, 0)
        up = mm(x, w_up, 1, 0)
        sigmoid = 1.0 / (1.0 + jnp.exp(-gate))
        active = gate * sigmoid
        hidden = (active * up).astype(BF16)
        made = mm(hidden, w_down, 1, 0).astype(BF16).astype(F32)
        ys[:, expert] = (made * prob).astype(BF16).reshape(SHARDS, SLOTS, D)
        ps[expert] = jnp.broadcast_to(
            jnp.sum(made * c, axis=1, keepdims=True), (ROWS, TPD)
        ).reshape(SHARDS, SLOTS, TPD)
        dmade = (prob * c).astype(BF16)
        dhidden = mm(dmade, w_down, 1, 1)
        dgate = (dhidden * up * (sigmoid + active * (1.0 - sigmoid))).astype(BF16)
        dup = (dhidden * active).astype(BF16)
        drows = mm(dgate, w_gate, 1, 1) + mm(dup, w_up, 1, 1)
        ds[:, expert] = drows.astype(BF16).reshape(SHARDS, SLOTS, D)
        for total_ref, before, left, right in zip(
            (gd_ref, gg_ref, gu_ref), before_refs, (hidden, x, x), (dmade, dgate, dup)
        ):
            term = mm(left, right, 0, 0)
            if later:
                term = term + before[0].astype(F32)
            total_ref[0] = term.astype(BF16)

    @pl.when(step >= PARTS + LOCAL_EXPERTS)
    def put():
        for k in range(PART):
            source = (step - PARTS - LOCAL_EXPERTS) * PART + k
            hots = [hot_of(e, source) for e in range(LOCAL_EXPERTS)]
            low = jnp.concatenate(hots, axis=0).astype(BF16)
            back_refs[k % 2][k // 2, :TPD] = mm(low, ds[source].reshape(-1, D), 0, 0).astype(BF16)
            out_refs[k % 2][k // 2] = mm(low, ys[source].reshape(-1, D), 0, 0).astype(BF16)
            pieces = []
            for e in range(LOCAL_EXPERTS):
                route = jnp.where(hots[e], ps[e, source], 0.0)
                route = jnp.sum(route, axis=0, keepdims=True)
                high = route.astype(BF16).astype(F32)
                pieces += [high, route - high]
            lanes = jnp.concatenate(pieces, axis=1)
            row = jnp.concatenate(
                [jnp.where(core_ref[0] == c, lanes, 0.0) for c in range(2)], axis=1
            )
            place = lax.broadcasted_iota(jnp.int32, (TALL - TPD, D), 0)
            back_refs[k % 2][k // 2, TPD:] = jnp.where(place == 0, row, 0.0).astype(BF16)


def experts_step(waits, core, rows, grads, slot, hit, router, w_gate, w_up, w_down, previous):
    later = previous is not None
    whole = lambda *shape: pl.BlockSpec(shape, lambda i, at: (0,) * len(shape))
    first = lambda i, at: (jnp.minimum(i, PARTS - 1), 0, 0)
    kinds = (len(rows), 1)
    second = lambda i, at: (jnp.minimum(i, PARTS - 1), 1 if later else 0, 0)
    last = lambda i, at: (jnp.maximum(i - PARTS - LOCAL_EXPERTS, 0), 0, 0)
    each = lambda *shape: pl.BlockSpec(
        (1, *shape), lambda i, at: (jnp.clip(i - PARTS, 0, LOCAL_EXPERTS - 1), 0, 0)
    )
    weight_specs = [each(D, FF), each(D, FF), each(FF, D)]
    shapes = [
        *[((CHIPS, TPD, D), BF16)] * 2,
        *[((CHIPS, TALL, D), BF16)] * 2,
        (w_gate.shape, BF16),
        (w_up.shape, BF16),
        (w_down.shape, BF16),
    ]
    return pl.pallas_call(
        functools.partial(expert_kernel, later=later, kinds=kinds, waits=len(waits)),
        grid_spec=pltpu.PrefetchScalarGridSpec(
            num_scalar_prefetch=1,
            grid=(2 * PARTS + LOCAL_EXPERTS,),
            in_specs=[
                *[pl.BlockSpec(memory_space=pl.ANY)] * len(waits),
                *[pl.BlockSpec((PART // len(rows), TPD, D), first)] * len(rows),
                pl.BlockSpec((PART, TPD, D), second),
            whole(LOCAL_EXPERTS, SHARDS, TPD),
            whole(SHARDS, EXPERTS, TPD),
            whole(EXPERTS, D),
        ]
        + weight_specs
        + (weight_specs if later else []),
        out_specs=[
            *[pl.BlockSpec((PART // 2, TPD, D), last)] * 2,
            *[pl.BlockSpec((PART // 2, TALL, D), last)] * 2,
        ]
        + weight_specs,
        scratch_shapes=[
            pltpu.VMEM((LOCAL_EXPERTS, SHARDS, SLOTS, D), BF16),
            pltpu.VMEM((LOCAL_EXPERTS, SHARDS, SLOTS, D), BF16),
            pltpu.VMEM((LOCAL_EXPERTS, SHARDS, SLOTS, TPD), F32),
            pltpu.VMEM((SHARDS, LOCAL_EXPERTS, SLOTS, D), BF16),
            pltpu.VMEM((SHARDS, LOCAL_EXPERTS, SLOTS, D), BF16),
        ],
        ),
        out_shape=[jax.ShapeDtypeStruct(shape, dtype) for shape, dtype in shapes],
        compiler_params=pltpu.CompilerParams(vmem_limit_bytes=60 * MIB),
        cost_estimate=BRIEF,
        name="experts",
    )(core, *waits, *rows, grads, slot, hit, router, w_gate, w_up, w_down, *(previous if later else ()))


def gather(values):
    return lax.all_gather(values, "shard", axis=0)


def nothing(values_ref, earlier_ref, out_ref):
    del values_ref, earlier_ref, out_ref


def after(values, earlier):
    anywhere = pl.BlockSpec(memory_space=pl.ANY)
    return pl.pallas_call(
        nothing,
        in_specs=[anywhere] * 2,
        out_specs=anywhere,
        out_shape=jax.ShapeDtypeStruct(values.shape, values.dtype),
        input_output_aliases={0: 0},
        cost_estimate=BRIEF,
        name="after",
    )(values, earlier)


Y_SWAP = [(index, (index + 8) % SHARDS) for index in range(SHARDS)]
X_SHIFTS = [
    [(index, index // 8 * 8 + (index + 2 * shift) % 8) for index in range(SHARDS)]
    for shift in range(1, 4)
]


def permute(values, pairs):
    return lax.ppermute(values, "shard", pairs)


def exchange(values, axis="shard", groups=None):
    return lax.all_to_all(
        values, axis, split_axis=0, concat_axis=0, tiled=True, axis_index_groups=groups
    )


def call(kernel, name, shapes, *operands, scalars=(), waits=(), specs=None):
    count, held = len(operands), len(scalars)
    specs = dict(specs or {})
    whole = lambda shape: pl.BlockSpec(shape, lambda i, *_: (0,) * len(shape))

    def body(*refs):
        kernel(*refs[: held + count], *refs[held + count + len(waits) :])

    return pl.pallas_call(
        body,
        grid_spec=pltpu.PrefetchScalarGridSpec(
            num_scalar_prefetch=held,
            grid=(1,),
            in_specs=[specs.get(i, whole(v.shape)) for i, v in enumerate(operands)]
            + [pl.BlockSpec(memory_space=pl.ANY)] * len(waits),
            out_specs=[whole(shape) for shape, _ in shapes],
        ),
        out_shape=[jax.ShapeDtypeStruct(shape, dtype) for shape, dtype in shapes],
        compiler_params=pltpu.CompilerParams(vmem_limit_bytes=60 * MIB),
        cost_estimate=BRIEF,
        name=name,
    )(*scalars, *operands, *waits)


def block(shape, *index):
    return pl.BlockSpec(shape, lambda i, *_: index)


OUT_ROWS = block((SHARDS, D // SHARDS, D), 0, 2, 0)


def mid_kernel(att_ref, wout_ref, x_ref, gain_ref, cot_ref, wqkv_ref, mid_ref, first_ref, second_ref):
    mid = x_ref[...].astype(F32) + mm(att_ref[...], wout_ref[...].reshape(HEADS * HD, D), 0, 0)
    mid_ref[...] = mid
    moe_in = (mid * rms_scale(mid) * gain_ref[...]).astype(BF16)
    first_ref[...] = jnp.broadcast_to(moe_in[None, :TPD], (CHIPS, TPD, D))
    own = D // SHARDS
    second_ref[:TPD] = moe_in[TPD:]
    second_ref[TPD : 2 * TPD] = cot_ref[TPD:]
    second_ref[2 * TPD : 2 * TPD + own] = wqkv_ref[:, :D]
    second_ref[2 * TPD + own :] = wqkv_ref[:, D:]


def add_kernel(x_ref, *refs, pairs):
    step = pl.program_id(0)
    del x_ref
    total = [
        (refs[2 * i][...].astype(F32) + refs[2 * i + 1][...].astype(F32)).astype(BF16)
        for i in range(pairs)
    ]
    out_refs = refs[2 * pairs :]
    if len(out_refs) == 1:
        out_refs[0][...] = total[0]
        return
    for k, out_ref in enumerate(out_refs):

        @pl.when(step == k)
        def put(out_ref=out_ref):
            for i in range(pairs):
                out_ref[i] = total[i][:, 0]


def sum_cores(keep, give):
    parts = 4
    spec = pl.BlockSpec((CHIPS // parts, *keep.shape[1:]), lambda i, at: (i, 0, 0))
    return pl.pallas_call(
        functools.partial(add_kernel, pairs=1),
        grid_spec=pltpu.PrefetchScalarGridSpec(
            num_scalar_prefetch=1, grid=(parts,), in_specs=[spec] * 2, out_specs=[spec]
        ),
        out_shape=[jax.ShapeDtypeStruct(keep.shape, BF16)],
        cost_estimate=BRIEF,
        name="sum_cores",
    )(jnp.zeros((1,), jnp.int32), keep, permute(give, OTHER_CORE))[0]


def sum_cores_by_x(pairs, shard):
    own = pairs[0][0].shape[1:]
    spec = pl.BlockSpec((2, 1, *own), lambda i, at: (0, (at[0] + i) % 4, 0, 0))
    shape = (len(pairs), 2, *own)
    whole = pl.BlockSpec(shape, lambda i, at: (0,) * len(shape))
    operands = []
    for keep, give in pairs:
        operands += [keep.reshape(2, 4, *own), permute(give, OTHER_CORE).reshape(2, 4, *own)]
    return pl.pallas_call(
        functools.partial(add_kernel, pairs=len(pairs)),
        grid_spec=pltpu.PrefetchScalarGridSpec(
            num_scalar_prefetch=1,
            grid=(4,),
            in_specs=[spec] * len(operands),
            out_specs=[whole] * 4,
        ),
        out_shape=[jax.ShapeDtypeStruct(shape, BF16)] * 4,
        compiler_params=pltpu.CompilerParams(vmem_limit_bytes=60 * MIB),
        cost_estimate=BRIEF,
        name="sum_cores_by_x",
    )((shard % 8 // 2).reshape(1), *operands)


def along_x_kernel(y_ref, a_ref, b_ref, c_ref, d_ref, keep_ref, give_ref):
    total = sum(ref[...].astype(F32) for ref in (a_ref, b_ref, c_ref, d_ref))
    own = y_ref[0] == 0
    keep_ref[...] = jnp.where(own, total[:, 0], total[:, 1])
    give_ref[...] = jnp.where(own, total[:, 1], total[:, 0]).astype(BF16)


def send_along_x(columns, wait):
    came = [permute(after(c, wait), shift) for c, shift in zip(columns[1:], X_SHIFTS)]
    return [columns[0], *came]


def sum_along_x(came, shard, wait):
    shape = (came[0].shape[0], *came[0].shape[2:])
    return call(
        along_x_kernel,
        "sum_along_x",
        [(shape, F32), (shape, BF16)],
        *came,
        scalars=[(shard // 8).reshape(1)],
        waits=(wait,),
    )


def expert_end_kernel(
    came_ref,
    mid_ref,
    cot_ref,
    router_ref,
    gain_ref,
    hit_ref,
    wout_ref,
    dmid_ref,
    low_ref,
    datt_ref,
    small_ref,
):
    dmoe_in = sum(came_ref[chip, :TPD].astype(F32) for chip in range(CHIPS))
    rows = []
    for chip in range(CHIPS):
        lanes = came_ref[chip, TPD:].astype(F32)[:1]
        for k in range(4):
            rows.append(
                lanes[:, 2 * k * TPD : (2 * k + 1) * TPD]
                + lanes[:, (2 * k + 1) * TPD : (2 * k + 2) * TPD]
            )
    route_grad = jnp.concatenate(rows, axis=0)
    mid = mid_ref[...]
    scale = rms_scale(mid)
    hat = mid * scale
    gain = gain_ref[...]
    rows_in = (hat * gain).astype(BF16)
    router = router_ref[...]
    gate = routed_softmax(mm(router, rows_in, 1, 1), hit_ref[...] > 0)
    dlogits = gate * (route_grad - jnp.sum(gate * route_grad, axis=0, keepdims=True))
    dlogits = dlogits.astype(BF16)
    dmoe_in = dmoe_in + mm(dlogits, router, 0, 0)
    small_ref[:EXPERTS] = mm(dlogits, rows_in, 1, 0)
    small_ref[EXPERTS:] = jnp.broadcast_to(
        jnp.sum(dmoe_in * hat, axis=0, keepdims=True), (8, D)
    )
    dmid = cot_ref[...].astype(F32) + norm_back(dmoe_in * gain, hat, scale)
    dmid_ref[...] = dmid
    low = dmid.astype(BF16)
    low_ref[...] = low
    datt = mm(wout_ref[...].reshape(HEADS * HD, D), low, 1, 1)
    datt_ref[...] = datt.astype(BF16).reshape(SHARDS, HD, TPD)


def out_kernel(core_ref, att_ref, first_ref, second_ref, keep_ref, give_ref):
    att = att_ref[...]
    total = mm(att[:, :TPD], first_ref[...], 1, 0) + mm(att[:, TPD:], second_ref[...], 1, 0)
    total = total.astype(BF16).reshape(CHIPS, 2, D // SHARDS, D)
    for core in range(2):

        @pl.when(core_ref[0] == core)
        def put(core=core):
            keep_ref[...] = total[:, core]
            give_ref[...] = total[:, 1 - core]


def input_kernel(dproj_ref, left_ref, right_ref, x_ref, dmid_ref, gain_ref, out_ref):
    queries = dproj_ref[:, :HD, :].reshape(HEADS * HD, TPD)
    paired = dproj_ref[:, HD:, :].astype(F32).reshape(KV_HEADS, 2, 2 * HD, TPD)
    paired = (paired[:, 0] + paired[:, 1]).astype(BF16)
    both = [paired[:, :HD].reshape(KV_HEADS * HD, TPD), paired[:, HD:].reshape(KV_HEADS * HD, TPD)]
    grad = mm(left_ref[...].reshape(D, D), queries, 1, 0)
    grad = grad + mm(right_ref[...].reshape(D, D), jnp.concatenate(both, axis=0), 1, 0)
    x = x_ref[...].astype(F32)
    scale = rms_scale(x)
    grad = norm_back(grad.T * gain_ref[...], x * scale, scale)
    out_ref[...] = (dmid_ref[...] + grad).astype(BF16)


def pack_kernel(ha_ref, hb_ref, sa_ref, sb_ref, ga_ref, gb_ref, out_ref):
    small = sa_ref[...] + sb_ref[...]
    gains = ga_ref[...] + gb_ref[...]
    lane = lax.broadcasted_iota(jnp.int32, (HD, D), 1)
    place = lax.broadcasted_iota(jnp.int32, (HD, D), 0)
    four = HD // SHARDS
    there = lane == place // four * (D // SHARDS) + place % four
    rows = [
        jnp.sum(jnp.where(there, gain[:, :1], 0.0), axis=0, keepdims=True)
        for gain in (gains[:HD], gains[HD:])
    ]
    rows = jnp.concatenate(
        [
            ha_ref[...] + hb_ref[...],
            small[: EXPERTS + 1],
            *rows,
            jnp.zeros((PACK - HEAD_COLS - EXPERTS - 3, D), F32),
        ],
        axis=0,
    )
    out_ref[...] = rows.T.astype(BF16).reshape(SHARDS, D // SHARDS, PACK)


def own_kernel(got_ref, keep_ref, came_ref, out_ref):
    left = lax.broadcasted_iota(jnp.int32, (D // SHARDS, TPD), 1) < HD
    swap = lambda v: pltpu.roll(v, HD, 1)
    query_key = [got_ref[h, :, :TPD].astype(F32) for h in range(HEADS)]
    value_rest = [got_ref[h, :, TPD:].astype(F32) for h in range(HEADS)]
    pairs = range(0, HEADS, 2)
    queries = [jnp.where(left, query_key[h], swap(query_key[h + 1])) for h in pairs]
    keys = [query_key[h] + query_key[h + 1] for h in pairs]
    values = [value_rest[h] + value_rest[h + 1] for h in pairs]
    rest = sum(values)
    keys = [jnp.where(left, swap(keys[h]), keys[h + 1]) for h in range(0, KV_HEADS, 2)]
    values = [jnp.where(left, values[h], swap(values[h + 1])) for h in range(0, KV_HEADS, 2)]
    out = keep_ref[...] + came_ref[...].astype(F32)
    out_ref[...] = jnp.concatenate([*queries, *keys, *values, out, rest], axis=1).astype(BF16)


def share_kernel(parts_ref, out_ref):
    total = sum(parts_ref[rep].astype(F32) for rep in range(REPS)).astype(BF16)
    out_ref[...] = jnp.broadcast_to(total[None], out_ref.shape)


def widen_kernel(*refs):
    for value_ref, out_ref in zip(refs[:3], refs[3:]):
        out_ref[...] = value_ref[...].astype(F32)


def widen(values):
    spec = lambda v: pl.BlockSpec((1, v.shape[1] // 2, v.shape[2]), lambda i: (i // 2, i % 2, 0))
    return pl.pallas_call(
        widen_kernel,
        grid=(2 * LOCAL_EXPERTS,),
        in_specs=[spec(v) for v in values],
        out_specs=[spec(v) for v in values],
        out_shape=[jax.ShapeDtypeStruct(v.shape, F32) for v in values],
        cost_estimate=BRIEF,
        name="widen",
    )(*values)


def last_kernel(all_ref, wqkv_ref, gain_ref, qkv_ref, out_ref, rest_ref):
    width = wqkv_ref.shape[1]
    rows = all_ref[...].astype(F32).reshape(D // SHARDS, -1)
    qkv_ref[...] = rows[:, :width]
    out_ref[...] = rows[:, width : width + D]
    gain = jnp.sum(rows[:, :width] * wqkv_ref[...].astype(F32), axis=1, keepdims=True)
    left = lax.broadcasted_iota(jnp.int32, (D // SHARDS, TPD), 1) < HD
    rest_ref[...] = jnp.where(left, gain / gain_ref[...], rows[:, width + D :])


def local(
    block_input,
    cotangent,
    routes,
    lengths,
    stream_slot,
    w_qkv,
    w_out,
    w_router,
    g_attn,
    g_moe,
    g_q,
    g_k,
    w_gate,
    w_up,
    w_down,
):
    shard = lax.axis_index("shard")
    core = shard % 2
    q_width = HEADS * HD
    kv_width = KV_HEADS * HD
    own_rows = D // SHARDS
    micro = lambda values, m: values[m * TPD : (m + 1) * TPD]

    x_all = gather(block_input)

    doubled = lambda part: jnp.repeat(part.reshape(own_rows, KV_HEADS, HD), 2, axis=1)
    column = lambda v: jnp.pad(v, (0, own_rows - v.shape[0]))[:, None]
    small = jnp.concatenate([w_router, column(g_attn), column(g_moe), column(g_q), column(g_k)], 1)
    small = jnp.pad(small, ((0, 0), (0, PACK - HEAD_COLS - small.shape[1])))
    packed = jnp.concatenate(
        [
            w_qkv[:, :q_width].reshape(own_rows, HEADS, HD),
            doubled(w_qkv[:, q_width : q_width + kv_width]),
            doubled(w_qkv[:, q_width + kv_width :]),
            jnp.broadcast_to(small[:, None], (own_rows, SHARDS, PACK - HEAD_COLS)),
        ],
        axis=2,
    )
    packed = exchange(packed.transpose(1, 0, 2))
    flat = packed.reshape(D, PACK)
    rest = flat[:, HEAD_COLS:].astype(F32)
    router = flat[:, HEAD_COLS : HEAD_COLS + EXPERTS]
    attn_gain = rest[:, EXPERTS][None]
    moe_gain = rest[:, EXPERTS + 1][None]
    quarter = rest.reshape(SHARDS, own_rows, -1)[:, : HD // SHARDS]
    query_gain = quarter[:, :, EXPERTS + 2].reshape(HD, 1)
    key_gain = quarter[:, :, EXPERTS + 3].reshape(HD, 1)

    freq = 10000.0 ** (-2.0 * jnp.arange(HALF, dtype=F32) / HD)
    earlier = jnp.triu(jnp.ones((TPD, TPD), BF16), 1)

    hits = []
    for m in range(MICRO):
        named = micro(routes, m).T
        hits.append(jnp.any(named[None] == jnp.arange(EXPERTS)[:, None, None], axis=1))
    extra = jnp.stack(hits).astype(BF16).reshape(MICRO * 4, D)
    extra = jnp.pad(extra, ((0, 16 - MICRO * 4), (0, 0)))
    ordered = jnp.arange(SHARDS) ^ core
    ends = jnp.cumsum(lengths[0], axis=1)
    stream = stream_slot[0][:, None, :]
    past = (stream >= ends[:, :, None]).astype(jnp.int32)
    seq_id = jnp.sum(past, axis=1, keepdims=True)
    position = stream - jnp.sum(past * lengths[0][:, :, None], axis=1, keepdims=True)
    angle = freq[:, None] * position.astype(F32)
    own = (seq_id == jnp.arange(SEQS)[:, None]).astype(F32)
    tables = jnp.concatenate([jnp.cos(angle), jnp.sin(angle), (own - 1.0) * APART, own], axis=1)
    tables = tables.reshape(MICRO, -1, CHUNKS, CHUNK).transpose(0, 2, 1, 3)
    for ready in (flat, tables):
        x_all = after(x_all, ready)
    packet = jnp.concatenate([micro(cotangent, 0), w_out, extra], axis=0)
    packet = gather(after(packet, x_all))
    hits_all = packet[:, TPD + own_rows :].reshape(SHARDS, 2 * MICRO, EXPERTS, TPD)
    hits_all = hits_all[:, :MICRO][ordered].transpose(1, 0, 2, 3)
    before = jnp.einsum("mset,tu->mseu", hits_all, earlier, preferred_element_type=F32)
    slot_all = jnp.where(hits_all > 0, before, -1.0)
    experts_own = shard * LOCAL_EXPERTS
    slot_all = lax.dynamic_slice_in_dim(slot_all, experts_own, LOCAL_EXPERTS, 2)
    slot_all = slot_all.transpose(0, 2, 1, 3)
    attn_in_all, raw, key, keyt, val, query, out, outf, inv = attn_fwd(
        x_all, flat, attn_gain, query_gain, key_gain, tables
    )
    attended = after(after(exchange(out), packet), slot_all).reshape(q_width, MICRO * TPD)
    mid, rows_first, rows_second = call(
        mid_kernel,
        "mid",
        [((MICRO * TPD, D), F32), ((CHIPS, TPD, D), BF16), ((3 * TPD, D), BF16)],
        attended,
        packet,
        block_input,
        moe_gain,
        cotangent,
        w_qkv,
        specs={1: OUT_ROWS},
    )
    rows_first = exchange(rows_first, groups=SAME_CORE)
    rows_first = (rows_first, permute(rows_first, OTHER_CORE))
    rows_second = gather(rows_second)

    own_experts = jnp.stack([core, experts_own])
    router_rows = router.T
    grads, sums, chips = None, [], []
    for m in range(MICRO):
        *parts, g_gate, g_up, g_down = experts_step(
            (chips[0],) if m else (),
            own_experts,
            (rows_second,) if m else rows_first,
            rows_second if m else packet,
            slot_all[m],
            hits_all[m].astype(F32),
            router_rows,
            w_gate,
            w_up,
            w_down,
            grads,
        )
        grads = (g_gate, g_up, g_down)
        sums.append(parts)
        if m == 0:
            chips.append(sum_cores(*parts[2:]))
            came = exchange(chips[0], groups=SAME_CORE)
    grad_experts = lax.psum(tuple(after(grad, came) for grad in grads), "rep")

    def expert_end(m, came):
        rows = block((TPD, D), m, 0)
        return call(
            expert_end_kernel,
            "expert_end",
            [
                ((TPD, D), F32),
                ((TPD, D), BF16),
                ((SHARDS, HD, TPD), BF16),
                ((EXPERTS + 8, D), F32),
            ],
            came,
            mid,
            cotangent,
            router_rows,
            moe_gain,
            hits[m].astype(F32),
            packet,
            specs={1: rows, 2: rows, 6: OUT_ROWS},
        )

    def attention_back(m, grad):
        return attn_bwd(
            m,
            grad,
            outf,
            inv,
            key,
            keyt,
            val,
            query,
            raw,
            attn_in_all,
            query_gain,
            key_gain,
            tables,
        )

    dmid_first, low_first, dattended, small_first = expert_end(0, came)

    def always(work):
        def none():
            return jax.tree.map(lambda v: jnp.zeros(v.shape, v.dtype), jax.eval_shape(work))

        return lax.cond(lengths[0, 0, 0] > 0, work, none)

    def back():
        grad_first = exchange(dattended)
        chip = sum_cores(*sums[1][2:])
        outs = sum_cores_by_x([parts[:2] for parts in sums], shard)
        chip = after(chip, grad_first)
        came = exchange(chip, groups=SAME_CORE)
        for ready in (chip, outs[0]):
            grad_first = after(grad_first, ready)
        dproj_first, head_first, gains_first = attention_back(0, grad_first)
        came = after(came, dproj_first)
        dmid_second, low_second, second, small_second = expert_end(1, came)
        keep, give = call(
            out_kernel,
            "out_part",
            [((CHIPS, own_rows, D), BF16)] * 2,
            attended,
            low_first,
            low_second,
            scalars=[core.reshape(1)],
        )
        out_own = sum_cores_by_x([(keep, give)], shard)
        second = after(exchange(second), out_own[0])
        dproj_first = after(dproj_first, second)
        out_own = send_along_x(out_own, second)
        second = after(second, dproj_first)
        dproj_second, head_second, gains_second = attention_back(1, second)
        dproj_first = exchange(dproj_first)
        keep, give = sum_along_x(out_own, shard, dproj_second)
        second_results = dproj_second, head_second, gains_second
        small = small_first, small_second
        first_results = dproj_first, head_first, gains_first
        return first_results, second_results, small, dmid_second, outs, keep, give

    first, second, small, dmid_second, outs, keep, give = always(back)
    dproj_first, head_first, gains_first = first
    dproj_second, head_second, gains_second = second
    small_first, small_second = small

    def send_gradients():
        (packed,) = call(
            pack_kernel,
            "pack",
            [((SHARDS, own_rows, PACK), BF16)],
            head_first,
            head_second,
            small_first,
            small_second,
            gains_first,
            gains_second,
        )
        dproj_all = [dproj_first, exchange(dproj_second)]
        for ready in (dproj_all[1],):
            packed = after(packed, ready)
        return dproj_all, exchange(packed)

    dproj_all, packed = always(send_gradients)
    outs = send_along_x(outs, packed)

    def finish():
        input_grads = []
        for m in range(MICRO):
            rows = block((TPD, D), m, 0)
            input_grads += call(
                input_kernel,
                "input_grad",
                [((TPD, D), BF16)],
                dproj_all[m],
                rows_second,
                rows_second,
                block_input,
                (dmid_first, dmid_second)[m],
                attn_gain,
                specs={
                    1: block((SHARDS, own_rows, D), 0, 4, 0),
                    2: block((SHARDS, own_rows, D), 0, 5, 0),
                    3: rows,
                },
            )
        width = q_width + 2 * kv_width
        (owned,) = call(
            own_kernel,
            "own",
            [((own_rows, width + D + TPD), BF16)],
            packed,
            keep[0],
            permute(give, Y_SWAP)[0],
        )
        owned = exchange(owned.reshape(REPS, own_rows // REPS, -1), "rep")
        (share,) = call(
            share_kernel, "share", [(owned.shape, BF16)], owned
        )
        grad_qkv, grad_out, rest = call(
            last_kernel,
            "last",
            [((own_rows, width), F32), ((own_rows, D), F32), ((own_rows, TPD), F32)],
            exchange(share, "rep"),
            w_qkv,
            g_attn.astype(F32)[:, None],
        )
        four = HD // SHARDS
        return (
            jnp.concatenate(input_grads, axis=0),
            grad_qkv,
            grad_out,
            rest[:, HD : HD + EXPERTS],
            rest[:, 0],
            rest[:, HD + EXPERTS],
            rest[:four, HD + EXPERTS + 1],
            rest[:four, HD + EXPERTS + 2],
        )

    results = always(finish)
    outs = sum_along_x(outs, shard, results[0])
    came = permute(outs[1], Y_SWAP)
    grad_experts = widen(grad_experts)
    output = outs[0] + after(came, grad_experts[0]).astype(F32)
    output = (mid + output.reshape(mid.shape)).astype(BF16)
    return (output, *results, *grad_experts)


def solution(mesh):
    rows = P(("rep", "shard"), None)
    rep, split, vector = P("rep", None, None), P("shard", None), P("shard")
    expert = P("shard", None, None)
    return jax.shard_map(
        local,
        mesh=mesh,
        in_specs=(rows,) * 3 + (rep,) * 2 + (split,) * 3 + (vector,) * 4 + (expert,) * 3,
        out_specs=(rows,) * 2 + (split,) * 3 + (vector,) * 4 + (expert,) * 3,
        check_vma=False,
    )
```

```python
import functools

import jax
import jax.numpy as jnp
from jax import lax
from jax.experimental import pallas as pl
from jax.experimental.pallas import tpu as pltpu
from jax.sharding import PartitionSpec as P

D = 1024
HEADS = 16
KV_HEADS = 8
HD = 64
HALF = HD // 2
FF = 512
TOP = 8
MICRO = 2
SEQS = 8
SHARDS = 16
REPS = 8
CHIPS = 8
TPD = 128
G = SHARDS * TPD
EXPERTS = 32
LOCAL_EXPERTS = EXPERTS // SHARDS
SLOTS = 48
ROWS = SHARDS * SLOTS
PART = 4
PARTS = SHARDS // PART
TALL = TPD + 16
CHUNK = 256
CHUNKS = G // CHUNK
SPAN = 1024
HEAD_COLS = 3 * HD
PACK = 256
APART = 256.0
EPS = 1e-06

F32 = jnp.float32
BF16 = jnp.bfloat16
MIB = 1 << 20

BRIEF = pl.CostEstimate(flops=1_000_000, bytes_accessed=1_000_000, transcendentals=0)

SAME_CORE = [[core + 2 * chip for chip in range(CHIPS)] for core in range(2)]
OTHER_CORE = [(index, index ^ 1) for index in range(SHARDS)]


def mm(a, b, left, right):
    return lax.dot_general(a, b, (((left,), (right,)), ((), ())), preferred_element_type=F32)


def rms_scale(values, axis=-1):
    return lax.rsqrt(jnp.mean(values * values, axis=axis, keepdims=True) + EPS)


def norm_back(grad_hat, normed, scale, axis=-1):
    return scale * (grad_hat - normed * jnp.mean(grad_hat * normed, axis=axis, keepdims=True))


def turn(values, cosine, sine):
    first, second = values[:HALF], values[HALF:]
    return jnp.concatenate(
        [first * cosine - second * sine, second * cosine + first * sine], axis=0
    )


def attn_fwd_kernel(
    x_ref,
    w_ref,
    ga_ref,
    gq_ref,
    gk_ref,
    tab_ref,
    ain_ref,
    raw_ref,
    key_ref,
    keyt_ref,
    val_ref,
    query_ref,
    out_ref,
    outf_ref,
    inv_ref,
    valt,
):
    step = pl.program_id(1)
    x = x_ref[...].reshape(SPAN, D).astype(F32)
    attn_in = (x * rms_scale(x) * ga_ref[...]).astype(BF16)
    ain_ref[0] = attn_in
    raw_all = mm(attn_in, w_ref[...], 1, 0).T
    pad = jnp.zeros((HD - SEQS, CHUNK), F32)
    place = lax.broadcasted_iota(jnp.int32, (HD, CHUNK), 0)
    for k in range(SPAN // CHUNK):
        chunk = step * (SPAN // CHUNK) + k
        tokens = pl.ds(pl.multiple_of(chunk * CHUNK, CHUNK), CHUNK)
        raw = raw_all[:, k * CHUNK : (k + 1) * CHUNK]
        raw_ref[0, chunk] = raw[: 2 * HD]
        table = tab_ref[0, chunk]
        cosine, sine = table[:HALF], table[HALF:HD]
        far, own = table[HD : HD + SEQS], table[HD + SEQS :]
        query_raw, key_raw, value = raw[:HD], raw[HD : 2 * HD], raw[2 * HD : HEAD_COLS]
        query = turn(query_raw * rms_scale(query_raw, 0) * gq_ref[...], cosine, sine).astype(BF16)
        key = turn(key_raw * rms_scale(key_raw, 0) * gk_ref[...], cosine, sine).astype(BF16)
        query_ref[0, chunk] = jnp.concatenate(
            [query.astype(F32) * HD**-0.5, far, pad], axis=0
        ).astype(BF16)
        keyt_ref[0, chunk] = key
        key_ref[0, tokens, :] = jnp.concatenate([key.astype(F32), own, pad], axis=0).T.astype(BF16)
        val_rows = jnp.concatenate([value, (place < 2).astype(F32)], axis=0)
        val_ref[0, tokens, :] = val_rows.T.astype(BF16)
        valt[:, tokens] = val_rows[: HD + 16].astype(BF16)

    @pl.when(step == G // SPAN - 1)
    def attend():
        tokens = pl.ds(pl.multiple_of(pl.program_id(0) * TPD, TPD), TPD)

        def one(j, carry):
            weights = jnp.exp(mm(key_ref[0], query_ref[0, j], 1, 0)).astype(BF16)
            total = mm(valt[...], weights, 1, 0)
            inv = 1.0 / total[HD : HD + 1]
            attended = total[:HD] * inv
            inv_ref[0, j] = inv
            outf_ref[0, j] = attended
            low = attended.astype(BF16)
            out_ref[2 * j, :, tokens] = low[:, :TPD]
            out_ref[2 * j + 1, :, tokens] = low[:, TPD:]
            return carry

        lax.fori_loop(0, CHUNKS, one, 0, unroll=True)


def attn_fwd(x_all, w_head, attn_gain, query_gain, key_gain, tables):
    whole = lambda *shape: pl.BlockSpec(shape, lambda m, i: (0,) * len(shape))
    each = lambda *shape: pl.BlockSpec((1, *shape), lambda m, i: (m,) + (0,) * len(shape))
    shapes = (
        ((MICRO, G, D), BF16),
        ((MICRO, CHUNKS, 2 * HD, CHUNK), F32),
        ((MICRO, G, 2 * HD), BF16),
        ((MICRO, CHUNKS, HD, CHUNK), BF16),
        ((MICRO, G, 2 * HD), BF16),
        ((MICRO, CHUNKS, 2 * HD, CHUNK), BF16),
        ((SHARDS, HD, MICRO * TPD), BF16),
        ((MICRO, CHUNKS, HD, CHUNK), F32),
        ((MICRO, CHUNKS, 1, CHUNK), F32),
    )
    return pl.pallas_call(
        attn_fwd_kernel,
        grid=(MICRO, G // SPAN),
        in_specs=[
            pl.BlockSpec((SPAN // TPD, TPD, D), lambda m, i: (i, m, 0)),
            whole(D, PACK),
            whole(1, D),
            whole(HD, 1),
            whole(HD, 1),
            each(CHUNKS, HD + 2 * SEQS, CHUNK),
        ],
        out_specs=[
            pl.BlockSpec((1, SPAN, D), lambda m, i: (m, i, 0)),
        ]
        + [each(*shape[1:]) for shape, _ in shapes[1:6]]
        + [whole(*shapes[6][0])]
        + [each(*shape[1:]) for shape, _ in shapes[7:]],
        out_shape=[jax.ShapeDtypeStruct(shape, dtype) for shape, dtype in shapes],
        scratch_shapes=[pltpu.VMEM((HD + 16, G), BF16)],
        compiler_params=pltpu.CompilerParams(vmem_limit_bytes=60 * MIB),
        cost_estimate=BRIEF,
        name="attn_fwd",
    )(x_all, w_head, attn_gain, query_gain, key_gain, tables)


def attn_bwd_kernel(
    grad_ref,
    outf_ref,
    inv_ref,
    key_ref,
    keyt_ref,
    val_ref,
    query_ref,
    raw_ref,
    ain_ref,
    gq_ref,
    gk_ref,
    tab_ref,
    dproj_ref,
    gw_ref,
    gain_ref,
    dq_s,
    dk_s,
    dv_s,
):
    keyt = jnp.concatenate([keyt_ref[0, j] for j in range(CHUNKS)], axis=1)
    dk_s[...] = jnp.zeros_like(dk_s)
    dv_s[...] = jnp.zeros_like(dv_s)
    pad = jnp.zeros((HD - 2, CHUNK), F32)

    def one(j, carry):
        grad = jnp.concatenate([grad_ref[2 * j], grad_ref[2 * j + 1]], axis=1).astype(F32)
        grad = grad * inv_ref[0, j]
        low = grad.astype(BF16)
        dot = -jnp.sum(low.astype(F32) * outf_ref[0, j], axis=0, keepdims=True)
        dot_high = dot.astype(BF16).astype(F32)
        rows = jnp.concatenate([grad, dot_high, dot - dot_high, pad], axis=0)
        query = query_ref[0, j]
        weights = jnp.exp(mm(key_ref[0], query, 1, 0))
        centred = mm(val_ref[0], rows.astype(BF16), 1, 0)
        dscores = (weights * centred).astype(BF16)
        dq_s[j] = mm(keyt, dscores, 1, 0) * HD**-0.5
        dk_s[...] += mm(dscores, query.astype(F32).T.astype(BF16), 1, 0)
        dv_s[...] += mm(weights.astype(BF16), rows.T.astype(BF16), 1, 0)
        return carry

    lax.fori_loop(0, CHUNKS, one, 0, unroll=True)
    gq, gk = gq_ref[...], gk_ref[...]
    gw_ref[...] = jnp.zeros_like(gw_ref)
    gain_ref[...] = jnp.zeros_like(gain_ref)

    def back(j, carry):
        tokens = pl.ds(j * CHUNK, CHUNK)
        cosine, sine = tab_ref[0, j, :HALF], -tab_ref[0, j, HALF:HD]
        raw = raw_ref[0, j]
        dk = dk_s[tokens, :].T[:HD]
        dv = dv_s[tokens, :].T[:HD]
        parts = []
        gains = []
        for grad, values, gain in ((dq_s[j], raw[:HD], gq), (dk, raw[HD:], gk)):
            normed_grad = turn(grad, cosine, sine)
            scale = rms_scale(values, 0)
            hat = values * scale
            gains.append(jnp.sum(normed_grad * hat, axis=1, keepdims=True))
            parts.append(norm_back(normed_grad * gain, hat, scale, 0))
        dproj = jnp.concatenate(parts + [dv], axis=0).astype(BF16)
        dproj_ref[2 * j] = dproj[:, :TPD]
        dproj_ref[2 * j + 1] = dproj[:, TPD:]
        gw_ref[...] += mm(dproj, ain_ref[0, tokens, :], 1, 0)
        gain_ref[...] += jnp.concatenate(
            [jnp.broadcast_to(g, (HD, TPD)) for g in gains], axis=0
        )
        return carry

    lax.fori_loop(0, CHUNKS, back, 0, unroll=2)


def attn_bwd(m, grad, *operands):
    shapes = (
        ((SHARDS, HEAD_COLS, TPD), BF16),
        ((HEAD_COLS, D), F32),
        ((2 * HD, TPD), F32),
    )
    whole = lambda *shape: pl.BlockSpec(shape, lambda i: (0,) * len(shape))
    each = lambda *shape: pl.BlockSpec((1, *shape), lambda i: (m,) + (0,) * len(shape))
    return pl.pallas_call(
        attn_bwd_kernel,
        grid=(1,),
        in_specs=[whole(*grad.shape)]
        + [each(*v.shape[1:]) if v.shape[0] == MICRO else whole(*v.shape) for v in operands],
        out_specs=[whole(*shape) for shape, _ in shapes],
        out_shape=[jax.ShapeDtypeStruct(shape, dtype) for shape, dtype in shapes],
        scratch_shapes=[
            pltpu.VMEM((CHUNKS, HD, CHUNK), F32),
            pltpu.VMEM((G, 2 * HD), F32),
            pltpu.VMEM((G, 2 * HD), F32),
        ],
        compiler_params=pltpu.CompilerParams(vmem_limit_bytes=60 * MIB),
        cost_estimate=BRIEF,
        name="attn_bwd",
    )(grad, *operands)


def routed_softmax(logits, hits):
    top = jnp.max(jnp.where(hits, logits, -jnp.inf), axis=0, keepdims=True)
    powers = jnp.where(hits, jnp.exp(jnp.where(hits, logits - top, 0.0)), 0.0)
    return powers / jnp.sum(powers, axis=0, keepdims=True)


def expert_kernel(core_ref, *refs, later, kinds, waits):
    refs = refs[waits:]
    rows_refs, refs = refs[: kinds[0]], refs[kinds[0] :]
    grads_refs, refs = refs[: kinds[1]], refs[kinds[1] :]
    slot_ref, hit_ref, router_ref, wg_ref, wu_ref, wd_ref, *refs = refs
    before_refs = (None,) * 3
    if later:
        before_refs = (refs[2], refs[0], refs[1])
        refs = refs[3:]
    out_refs, back_refs = refs[:2], refs[2:4]
    gg_ref, gu_ref, gd_ref = refs[4:7]
    xs, cs, ps, ys, ds = refs[7:]
    step = pl.program_id(0)
    slots = lax.broadcasted_iota(jnp.int32, (SLOTS, TPD), 0).astype(F32)

    def block(refs, k):
        if len(refs) == 2:
            return refs[k % 2][k // 2]
        return refs[0][k ^ core_ref[0]]

    def hot_of(expert, source):
        return slots == slot_ref[expert, pl.ds(source, 1), :]

    @pl.when(step < PARTS)
    def pick():
        for k in range(PART):
            source = step * PART + k
            hots = [hot_of(e, source) for e in range(LOCAL_EXPERTS)]
            low = jnp.concatenate(hots, axis=0).astype(BF16)
            shape = (LOCAL_EXPERTS, SLOTS, D)
            rows = block(rows_refs, k)
            xs[:, source] = mm(low, rows, 1, 0).astype(BF16).reshape(shape)
            cs[:, source] = mm(low, block(grads_refs, k), 1, 0).astype(BF16).reshape(shape)
            gates = routed_softmax(mm(router_ref[...], rows, 1, 1), hit_ref[source] > 0)
            named = lax.broadcasted_iota(jnp.int32, (EXPERTS, TPD), 0) - core_ref[1]
            for e in range(LOCAL_EXPERTS):
                gate = jnp.sum(jnp.where(named == e, gates, 0.0), axis=0, keepdims=True)
                gate = jnp.where(hots[e], gate, 0.0)
                ps[e, source] = jnp.broadcast_to(
                    jnp.sum(gate, axis=1, keepdims=True), (SLOTS, TPD)
                )

    @pl.when((step >= PARTS) & (step < PARTS + LOCAL_EXPERTS))
    def work():
        expert = step - PARTS
        w_gate, w_up, w_down = wg_ref[0], wu_ref[0], wd_ref[0]
        x = xs[expert].reshape(ROWS, D)
        c = cs[expert].reshape(ROWS, D).astype(F32)
        prob = ps[expert].reshape(ROWS, TPD)[:, :1]
        gate = mm(x, w_gate, 1, 0)
        up = mm(x, w_up, 1, 0)
        sigmoid = 1.0 / (1.0 + jnp.exp(-gate))
        active = gate * sigmoid
        hidden = (active * up).astype(BF16)
        made = mm(hidden, w_down, 1, 0).astype(BF16).astype(F32)
        ys[:, expert] = (made * prob).astype(BF16).reshape(SHARDS, SLOTS, D)
        ps[expert] = jnp.broadcast_to(
            jnp.sum(made * c, axis=1, keepdims=True), (ROWS, TPD)
        ).reshape(SHARDS, SLOTS, TPD)
        dmade = (prob * c).astype(BF16)
        dhidden = mm(dmade, w_down, 1, 1)
        dgate = (dhidden * up * (sigmoid + active * (1.0 - sigmoid))).astype(BF16)
        dup = (dhidden * active).astype(BF16)
        drows = mm(dgate, w_gate, 1, 1) + mm(dup, w_up, 1, 1)
        ds[:, expert] = drows.astype(BF16).reshape(SHARDS, SLOTS, D)
        for total_ref, before, left, right in zip(
            (gd_ref, gg_ref, gu_ref), before_refs, (hidden, x, x), (dmade, dgate, dup)
        ):
            term = mm(left, right, 0, 0)
            if later:
                term = term + before[0].astype(F32)
            total_ref[0] = term.astype(BF16)

    @pl.when(step >= PARTS + LOCAL_EXPERTS)
    def put():
        for k in range(PART):
            source = (step - PARTS - LOCAL_EXPERTS) * PART + k
            hots = [hot_of(e, source) for e in range(LOCAL_EXPERTS)]
            low = jnp.concatenate(hots, axis=0).astype(BF16)
            back_refs[k % 2][k // 2, :TPD] = mm(low, ds[source].reshape(-1, D), 0, 0).astype(BF16)
            out_refs[k % 2][k // 2] = mm(low, ys[source].reshape(-1, D), 0, 0).astype(BF16)
            pieces = []
            for e in range(LOCAL_EXPERTS):
                route = jnp.where(hots[e], ps[e, source], 0.0)
                route = jnp.sum(route, axis=0, keepdims=True)
                high = route.astype(BF16).astype(F32)
                pieces += [high, route - high]
            lanes = jnp.concatenate(pieces, axis=1)
            row = jnp.concatenate(
                [jnp.where(core_ref[0] == c, lanes, 0.0) for c in range(2)], axis=1
            )
            place = lax.broadcasted_iota(jnp.int32, (TALL - TPD, D), 0)
            back_refs[k % 2][k // 2, TPD:] = jnp.where(place == 0, row, 0.0).astype(BF16)


def experts_step(waits, core, rows, grads, slot, hit, router, w_gate, w_up, w_down, previous):
    later = previous is not None
    whole = lambda *shape: pl.BlockSpec(shape, lambda i, at: (0,) * len(shape))
    first = lambda i, at: (jnp.minimum(i, PARTS - 1), 0, 0)
    kinds = (len(rows), 1)
    second = lambda i, at: (jnp.minimum(i, PARTS - 1), 1 if later else 0, 0)
    last = lambda i, at: (jnp.maximum(i - PARTS - LOCAL_EXPERTS, 0), 0, 0)
    each = lambda *shape: pl.BlockSpec(
        (1, *shape), lambda i, at: (jnp.clip(i - PARTS, 0, LOCAL_EXPERTS - 1), 0, 0)
    )
    weight_specs = [each(D, FF), each(D, FF), each(FF, D)]
    shapes = [
        *[((CHIPS, TPD, D), BF16)] * 2,
        *[((CHIPS, TALL, D), BF16)] * 2,
        (w_gate.shape, BF16),
        (w_up.shape, BF16),
        (w_down.shape, BF16),
    ]
    return pl.pallas_call(
        functools.partial(expert_kernel, later=later, kinds=kinds, waits=len(waits)),
        grid_spec=pltpu.PrefetchScalarGridSpec(
            num_scalar_prefetch=1,
            grid=(2 * PARTS + LOCAL_EXPERTS,),
            in_specs=[
                *[pl.BlockSpec(memory_space=pl.ANY)] * len(waits),
                *[pl.BlockSpec((PART // len(rows), TPD, D), first)] * len(rows),
                pl.BlockSpec((PART, TPD, D), second),
            whole(LOCAL_EXPERTS, SHARDS, TPD),
            whole(SHARDS, EXPERTS, TPD),
            whole(EXPERTS, D),
        ]
        + weight_specs
        + (weight_specs if later else []),
        out_specs=[
            *[pl.BlockSpec((PART // 2, TPD, D), last)] * 2,
            *[pl.BlockSpec((PART // 2, TALL, D), last)] * 2,
        ]
        + weight_specs,
        scratch_shapes=[
            pltpu.VMEM((LOCAL_EXPERTS, SHARDS, SLOTS, D), BF16),
            pltpu.VMEM((LOCAL_EXPERTS, SHARDS, SLOTS, D), BF16),
            pltpu.VMEM((LOCAL_EXPERTS, SHARDS, SLOTS, TPD), F32),
            pltpu.VMEM((SHARDS, LOCAL_EXPERTS, SLOTS, D), BF16),
            pltpu.VMEM((SHARDS, LOCAL_EXPERTS, SLOTS, D), BF16),
        ],
        ),
        out_shape=[jax.ShapeDtypeStruct(shape, dtype) for shape, dtype in shapes],
        compiler_params=pltpu.CompilerParams(vmem_limit_bytes=60 * MIB),
        cost_estimate=BRIEF,
        name="experts",
    )(core, *waits, *rows, grads, slot, hit, router, w_gate, w_up, w_down, *(previous if later else ()))


def gather(values):
    return lax.all_gather(values, "shard", axis=0)


def nothing(values_ref, earlier_ref, out_ref):
    del values_ref, earlier_ref, out_ref


def after(values, earlier):
    anywhere = pl.BlockSpec(memory_space=pl.ANY)
    return pl.pallas_call(
        nothing,
        in_specs=[anywhere] * 2,
        out_specs=anywhere,
        out_shape=jax.ShapeDtypeStruct(values.shape, values.dtype),
        input_output_aliases={0: 0},
        cost_estimate=BRIEF,
        name="after",
    )(values, earlier)


Y_SWAP = [(index, (index + 8) % SHARDS) for index in range(SHARDS)]
X_SHIFTS = [
    [(index, index // 8 * 8 + (index + 2 * shift) % 8) for index in range(SHARDS)]
    for shift in range(1, 4)
]


def permute(values, pairs):
    return lax.ppermute(values, "shard", pairs)


def exchange(values, axis="shard", groups=None):
    return lax.all_to_all(
        values, axis, split_axis=0, concat_axis=0, tiled=True, axis_index_groups=groups
    )


def call(kernel, name, shapes, *operands, scalars=(), waits=(), specs=None):
    count, held = len(operands), len(scalars)
    specs = dict(specs or {})
    whole = lambda shape: pl.BlockSpec(shape, lambda i, *_: (0,) * len(shape))

    def body(*refs):
        kernel(*refs[: held + count], *refs[held + count + len(waits) :])

    return pl.pallas_call(
        body,
        grid_spec=pltpu.PrefetchScalarGridSpec(
            num_scalar_prefetch=held,
            grid=(1,),
            in_specs=[specs.get(i, whole(v.shape)) for i, v in enumerate(operands)]
            + [pl.BlockSpec(memory_space=pl.ANY)] * len(waits),
            out_specs=[whole(shape) for shape, _ in shapes],
        ),
        out_shape=[jax.ShapeDtypeStruct(shape, dtype) for shape, dtype in shapes],
        compiler_params=pltpu.CompilerParams(vmem_limit_bytes=60 * MIB),
        cost_estimate=BRIEF,
        name=name,
    )(*scalars, *operands, *waits)


def block(shape, *index):
    return pl.BlockSpec(shape, lambda i, *_: index)


OUT_ROWS = block((SHARDS, D // SHARDS, D), 0, 2, 0)


def mid_kernel(att_ref, wout_ref, x_ref, gain_ref, cot_ref, wqkv_ref, mid_ref, first_ref, second_ref):
    mid = x_ref[...].astype(F32) + mm(att_ref[...], wout_ref[...].reshape(HEADS * HD, D), 0, 0)
    mid_ref[...] = mid
    moe_in = (mid * rms_scale(mid) * gain_ref[...]).astype(BF16)
    first_ref[...] = jnp.broadcast_to(moe_in[None, :TPD], (CHIPS, TPD, D))
    own = D // SHARDS
    second_ref[:TPD] = moe_in[TPD:]
    second_ref[TPD : 2 * TPD] = cot_ref[TPD:]
    second_ref[2 * TPD : 2 * TPD + own] = wqkv_ref[:, :D]
    second_ref[2 * TPD + own :] = wqkv_ref[:, D:]


def add_kernel(x_ref, *refs, pairs):
    step = pl.program_id(0)
    del x_ref
    total = [
        (refs[2 * i][...].astype(F32) + refs[2 * i + 1][...].astype(F32)).astype(BF16)
        for i in range(pairs)
    ]
    out_refs = refs[2 * pairs :]
    if len(out_refs) == 1:
        out_refs[0][...] = total[0]
        return
    for k, out_ref in enumerate(out_refs):

        @pl.when(step == k)
        def put(out_ref=out_ref):
            for i in range(pairs):
                out_ref[i] = total[i][:, 0]


def sum_cores(keep, give):
    parts = 2
    spec = pl.BlockSpec((CHIPS // parts, *keep.shape[1:]), lambda i, at: (i, 0, 0))
    return pl.pallas_call(
        functools.partial(add_kernel, pairs=1),
        grid_spec=pltpu.PrefetchScalarGridSpec(
            num_scalar_prefetch=1, grid=(parts,), in_specs=[spec] * 2, out_specs=[spec]
        ),
        out_shape=[jax.ShapeDtypeStruct(keep.shape, BF16)],
        cost_estimate=BRIEF,
        name="sum_cores",
    )(jnp.zeros((1,), jnp.int32), keep, permute(give, OTHER_CORE))[0]


def sum_cores_by_x(pairs, shard):
    own = pairs[0][0].shape[1:]
    spec = pl.BlockSpec((2, 1, *own), lambda i, at: (0, (at[0] + i) % 4, 0, 0))
    shape = (len(pairs), 2, *own)
    whole = pl.BlockSpec(shape, lambda i, at: (0,) * len(shape))
    operands = []
    for keep, give in pairs:
        operands += [keep.reshape(2, 4, *own), permute(give, OTHER_CORE).reshape(2, 4, *own)]
    return pl.pallas_call(
        functools.partial(add_kernel, pairs=len(pairs)),
        grid_spec=pltpu.PrefetchScalarGridSpec(
            num_scalar_prefetch=1,
            grid=(4,),
            in_specs=[spec] * len(operands),
            out_specs=[whole] * 4,
        ),
        out_shape=[jax.ShapeDtypeStruct(shape, BF16)] * 4,
        compiler_params=pltpu.CompilerParams(vmem_limit_bytes=60 * MIB),
        cost_estimate=BRIEF,
        name="sum_cores_by_x",
    )((shard % 8 // 2).reshape(1), *operands)


def along_x_kernel(y_ref, a_ref, b_ref, c_ref, d_ref, keep_ref, give_ref):
    total = sum(ref[...].astype(F32) for ref in (a_ref, b_ref, c_ref, d_ref))
    own = y_ref[0] == 0
    keep_ref[...] = jnp.where(own, total[:, 0], total[:, 1])
    give_ref[...] = jnp.where(own, total[:, 1], total[:, 0]).astype(BF16)


def send_along_x(columns, wait):
    came = [permute(after(c, wait), shift) for c, shift in zip(columns[1:], X_SHIFTS)]
    return [columns[0], *came]


def sum_along_x(came, shard, wait):
    shape = (came[0].shape[0], *came[0].shape[2:])
    return call(
        along_x_kernel,
        "sum_along_x",
        [(shape, F32), (shape, BF16)],
        *came,
        scalars=[(shard // 8).reshape(1)],
        waits=(wait,),
    )


def expert_end_kernel(
    came_ref,
    mid_ref,
    cot_ref,
    router_ref,
    gain_ref,
    hit_ref,
    wout_ref,
    dmid_ref,
    low_ref,
    datt_ref,
    small_ref,
):
    dmoe_in = sum(came_ref[chip, :TPD].astype(F32) for chip in range(CHIPS))
    rows = []
    for chip in range(CHIPS):
        lanes = came_ref[chip, TPD:].astype(F32)[:1]
        for k in range(4):
            rows.append(
                lanes[:, 2 * k * TPD : (2 * k + 1) * TPD]
                + lanes[:, (2 * k + 1) * TPD : (2 * k + 2) * TPD]
            )
    route_grad = jnp.concatenate(rows, axis=0)
    mid = mid_ref[...]
    scale = rms_scale(mid)
    hat = mid * scale
    gain = gain_ref[...]
    rows_in = (hat * gain).astype(BF16)
    router = router_ref[...]
    gate = routed_softmax(mm(router, rows_in, 1, 1), hit_ref[...] > 0)
    dlogits = gate * (route_grad - jnp.sum(gate * route_grad, axis=0, keepdims=True))
    dlogits = dlogits.astype(BF16)
    dmoe_in = dmoe_in + mm(dlogits, router, 0, 0)
    small_ref[:EXPERTS] = mm(dlogits, rows_in, 1, 0)
    small_ref[EXPERTS:] = jnp.broadcast_to(
        jnp.sum(dmoe_in * hat, axis=0, keepdims=True), (8, D)
    )
    dmid = cot_ref[...].astype(F32) + norm_back(dmoe_in * gain, hat, scale)
    dmid_ref[...] = dmid
    low = dmid.astype(BF16)
    low_ref[...] = low
    datt = mm(wout_ref[...].reshape(HEADS * HD, D), low, 1, 1)
    datt_ref[...] = datt.astype(BF16).reshape(SHARDS, HD, TPD)


def out_kernel(core_ref, att_ref, first_ref, second_ref, keep_ref, give_ref):
    att = att_ref[...]
    total = mm(att[:, :TPD], first_ref[...], 1, 0) + mm(att[:, TPD:], second_ref[...], 1, 0)
    total = total.astype(BF16).reshape(CHIPS, 2, D // SHARDS, D)
    for core in range(2):

        @pl.when(core_ref[0] == core)
        def put(core=core):
            keep_ref[...] = total[:, core]
            give_ref[...] = total[:, 1 - core]


def input_kernel(dproj_ref, left_ref, right_ref, x_ref, dmid_ref, gain_ref, out_ref):
    queries = dproj_ref[:, :HD, :].reshape(HEADS * HD, TPD)
    paired = dproj_ref[:, HD:, :].astype(F32).reshape(KV_HEADS, 2, 2 * HD, TPD)
    paired = (paired[:, 0] + paired[:, 1]).astype(BF16)
    both = [paired[:, :HD].reshape(KV_HEADS * HD, TPD), paired[:, HD:].reshape(KV_HEADS * HD, TPD)]
    grad = mm(left_ref[...].reshape(D, D), queries, 1, 0)
    grad = grad + mm(right_ref[...].reshape(D, D), jnp.concatenate(both, axis=0), 1, 0)
    x = x_ref[...].astype(F32)
    scale = rms_scale(x)
    grad = norm_back(grad.T * gain_ref[...], x * scale, scale)
    out_ref[...] = (dmid_ref[...] + grad).astype(BF16)


def pack_kernel(ha_ref, hb_ref, sa_ref, sb_ref, ga_ref, gb_ref, out_ref):
    small = sa_ref[...] + sb_ref[...]
    gains = ga_ref[...] + gb_ref[...]
    lane = lax.broadcasted_iota(jnp.int32, (HD, D), 1)
    place = lax.broadcasted_iota(jnp.int32, (HD, D), 0)
    four = HD // SHARDS
    there = lane == place // four * (D // SHARDS) + place % four
    rows = [
        jnp.sum(jnp.where(there, gain[:, :1], 0.0), axis=0, keepdims=True)
        for gain in (gains[:HD], gains[HD:])
    ]
    rows = jnp.concatenate(
        [
            ha_ref[...] + hb_ref[...],
            small[: EXPERTS + 1],
            *rows,
            jnp.zeros((PACK - HEAD_COLS - EXPERTS - 3, D), F32),
        ],
        axis=0,
    )
    out_ref[...] = rows.T.astype(BF16).reshape(SHARDS, D // SHARDS, PACK)


def own_kernel(got_ref, keep_ref, came_ref, out_ref):
    left = lax.broadcasted_iota(jnp.int32, (D // SHARDS, TPD), 1) < HD
    swap = lambda v: pltpu.roll(v, HD, 1)
    query_key = [got_ref[h, :, :TPD].astype(F32) for h in range(HEADS)]
    value_rest = [got_ref[h, :, TPD:].astype(F32) for h in range(HEADS)]
    pairs = range(0, HEADS, 2)
    queries = [jnp.where(left, query_key[h], swap(query_key[h + 1])) for h in pairs]
    keys = [query_key[h] + query_key[h + 1] for h in pairs]
    values = [value_rest[h] + value_rest[h + 1] for h in pairs]
    rest = sum(values)
    keys = [jnp.where(left, swap(keys[h]), keys[h + 1]) for h in range(0, KV_HEADS, 2)]
    values = [jnp.where(left, values[h], swap(values[h + 1])) for h in range(0, KV_HEADS, 2)]
    out = keep_ref[...] + came_ref[...].astype(F32)
    out_ref[...] = jnp.concatenate([*queries, *keys, *values, out, rest], axis=1).astype(BF16)


def share_kernel(parts_ref, out_ref):
    total = sum(parts_ref[rep].astype(F32) for rep in range(REPS)).astype(BF16)
    out_ref[...] = jnp.broadcast_to(total[None], out_ref.shape)


def widen_kernel(*refs):
    for value_ref, out_ref in zip(refs[:3], refs[3:]):
        out_ref[...] = value_ref[...].astype(F32)


def widen(values):
    spec = lambda v: pl.BlockSpec((1, v.shape[1] // 2, v.shape[2]), lambda i: (i // 2, i % 2, 0))
    return pl.pallas_call(
        widen_kernel,
        grid=(2 * LOCAL_EXPERTS,),
        in_specs=[spec(v) for v in values],
        out_specs=[spec(v) for v in values],
        out_shape=[jax.ShapeDtypeStruct(v.shape, F32) for v in values],
        cost_estimate=BRIEF,
        name="widen",
    )(*values)


def last_kernel(all_ref, wqkv_ref, gain_ref, qkv_ref, out_ref, rest_ref):
    width = wqkv_ref.shape[1]
    rows = all_ref[...].astype(F32).reshape(D // SHARDS, -1)
    qkv_ref[...] = rows[:, :width]
    out_ref[...] = rows[:, width : width + D]
    gain = jnp.sum(rows[:, :width] * wqkv_ref[...].astype(F32), axis=1, keepdims=True)
    left = lax.broadcasted_iota(jnp.int32, (D // SHARDS, TPD), 1) < HD
    rest_ref[...] = jnp.where(left, gain / gain_ref[...], rows[:, width + D :])


def local(
    block_input,
    cotangent,
    routes,
    lengths,
    stream_slot,
    w_qkv,
    w_out,
    w_router,
    g_attn,
    g_moe,
    g_q,
    g_k,
    w_gate,
    w_up,
    w_down,
):
    shard = lax.axis_index("shard")
    core = shard % 2
    q_width = HEADS * HD
    kv_width = KV_HEADS * HD
    own_rows = D // SHARDS
    micro = lambda values, m: values[m * TPD : (m + 1) * TPD]

    x_all = gather(block_input)

    doubled = lambda part: jnp.repeat(part.reshape(own_rows, KV_HEADS, HD), 2, axis=1)
    column = lambda v: jnp.pad(v, (0, own_rows - v.shape[0]))[:, None]
    small = jnp.concatenate([w_router, column(g_attn), column(g_moe), column(g_q), column(g_k)], 1)
    small = jnp.pad(small, ((0, 0), (0, PACK - HEAD_COLS - small.shape[1])))
    packed = jnp.concatenate(
        [
            w_qkv[:, :q_width].reshape(own_rows, HEADS, HD),
            doubled(w_qkv[:, q_width : q_width + kv_width]),
            doubled(w_qkv[:, q_width + kv_width :]),
            jnp.broadcast_to(small[:, None], (own_rows, SHARDS, PACK - HEAD_COLS)),
        ],
        axis=2,
    )
    packed = exchange(packed.transpose(1, 0, 2))
    flat = packed.reshape(D, PACK)
    rest = flat[:, HEAD_COLS:].astype(F32)
    router = flat[:, HEAD_COLS : HEAD_COLS + EXPERTS]
    attn_gain = rest[:, EXPERTS][None]
    moe_gain = rest[:, EXPERTS + 1][None]
    quarter = rest.reshape(SHARDS, own_rows, -1)[:, : HD // SHARDS]
    query_gain = quarter[:, :, EXPERTS + 2].reshape(HD, 1)
    key_gain = quarter[:, :, EXPERTS + 3].reshape(HD, 1)

    freq = 10000.0 ** (-2.0 * jnp.arange(HALF, dtype=F32) / HD)
    earlier = jnp.triu(jnp.ones((TPD, TPD), BF16), 1)

    hits = []
    for m in range(MICRO):
        named = micro(routes, m).T
        hits.append(jnp.any(named[None] == jnp.arange(EXPERTS)[:, None, None], axis=1))
    extra = jnp.stack(hits).astype(BF16).reshape(MICRO * 4, D)
    extra = jnp.pad(extra, ((0, 16 - MICRO * 4), (0, 0)))
    ordered = jnp.arange(SHARDS) ^ core
    ends = jnp.cumsum(lengths[0], axis=1)
    stream = stream_slot[0][:, None, :]
    past = (stream >= ends[:, :, None]).astype(jnp.int32)
    seq_id = jnp.sum(past, axis=1, keepdims=True)
    position = stream - jnp.sum(past * lengths[0][:, :, None], axis=1, keepdims=True)
    angle = freq[:, None] * position.astype(F32)
    own = (seq_id == jnp.arange(SEQS)[:, None]).astype(F32)
    tables = jnp.concatenate([jnp.cos(angle), jnp.sin(angle), (own - 1.0) * APART, own], axis=1)
    tables = tables.reshape(MICRO, -1, CHUNKS, CHUNK).transpose(0, 2, 1, 3)
    for ready in (flat, tables):
        x_all = after(x_all, ready)
    packet = jnp.concatenate([micro(cotangent, 0), w_out, extra], axis=0)
    packet = gather(after(packet, x_all))
    hits_all = packet[:, TPD + own_rows :].reshape(SHARDS, 2 * MICRO, EXPERTS, TPD)
    hits_all = hits_all[:, :MICRO][ordered].transpose(1, 0, 2, 3)
    before = jnp.einsum("mset,tu->mseu", hits_all, earlier, preferred_element_type=F32)
    slot_all = jnp.where(hits_all > 0, before, -1.0)
    experts_own = shard * LOCAL_EXPERTS
    slot_all = lax.dynamic_slice_in_dim(slot_all, experts_own, LOCAL_EXPERTS, 2)
    slot_all = slot_all.transpose(0, 2, 1, 3)
    attn_in_all, raw, key, keyt, val, query, out, outf, inv = attn_fwd(
        x_all, flat, attn_gain, query_gain, key_gain, tables
    )
    attended = after(after(exchange(out), packet), slot_all).reshape(q_width, MICRO * TPD)
    mid, rows_first, rows_second = call(
        mid_kernel,
        "mid",
        [((MICRO * TPD, D), F32), ((CHIPS, TPD, D), BF16), ((3 * TPD, D), BF16)],
        attended,
        packet,
        block_input,
        moe_gain,
        cotangent,
        w_qkv,
        specs={1: OUT_ROWS},
    )
    rows_first = exchange(rows_first, groups=SAME_CORE)
    rows_first = (rows_first, permute(rows_first, OTHER_CORE))
    rows_second = gather(rows_second)

    own_experts = jnp.stack([core, experts_own])
    router_rows = router.T
    grads, sums, chips = None, [], []
    for m in range(MICRO):
        *parts, g_gate, g_up, g_down = experts_step(
            (chips[0],) if m else (),
            own_experts,
            (rows_second,) if m else rows_first,
            rows_second if m else packet,
            slot_all[m],
            hits_all[m].astype(F32),
            router_rows,
            w_gate,
            w_up,
            w_down,
            grads,
        )
        grads = (g_gate, g_up, g_down)
        sums.append(parts)
        if m == 0:
            chips.append(sum_cores(*parts[2:]))
            came = exchange(chips[0], groups=SAME_CORE)
    grad_experts = lax.psum(tuple(after(grad, came) for grad in grads), "rep")

    def expert_end(m, came):
        rows = block((TPD, D), m, 0)
        return call(
            expert_end_kernel,
            "expert_end",
            [
                ((TPD, D), F32),
                ((TPD, D), BF16),
                ((SHARDS, HD, TPD), BF16),
                ((EXPERTS + 8, D), F32),
            ],
            came,
            mid,
            cotangent,
            router_rows,
            moe_gain,
            hits[m].astype(F32),
            packet,
            specs={1: rows, 2: rows, 6: OUT_ROWS},
        )

    def attention_back(m, grad):
        return attn_bwd(
            m,
            grad,
            outf,
            inv,
            key,
            keyt,
            val,
            query,
            raw,
            attn_in_all,
            query_gain,
            key_gain,
            tables,
        )

    dmid_first, low_first, dattended, small_first = expert_end(0, came)

    def always(work):
        def none():
            return jax.tree.map(lambda v: jnp.zeros(v.shape, v.dtype), jax.eval_shape(work))

        return lax.cond(lengths[0, 0, 0] > 0, work, none)

    def back():
        grad_first = exchange(dattended)
        chip = sum_cores(*sums[1][2:])
        outs = sum_cores_by_x([parts[:2] for parts in sums], shard)
        chip = after(chip, grad_first)
        came = exchange(chip, groups=SAME_CORE)
        for ready in (chip, outs[0]):
            grad_first = after(grad_first, ready)
        dproj_first, head_first, gains_first = attention_back(0, grad_first)
        came = after(came, dproj_first)
        dmid_second, low_second, second, small_second = expert_end(1, came)
        keep, give = call(
            out_kernel,
            "out_part",
            [((CHIPS, own_rows, D), BF16)] * 2,
            attended,
            low_first,
            low_second,
            scalars=[core.reshape(1)],
        )
        out_own = sum_cores_by_x([(keep, give)], shard)
        second = after(exchange(second), out_own[0])
        dproj_first = after(dproj_first, second)
        out_own = send_along_x(out_own, second)
        second = after(second, dproj_first)
        dproj_second, head_second, gains_second = attention_back(1, second)
        dproj_first = exchange(dproj_first)
        keep, give = sum_along_x(out_own, shard, dproj_second)
        second_results = dproj_second, head_second, gains_second
        small = small_first, small_second
        first_results = dproj_first, head_first, gains_first
        return first_results, second_results, small, dmid_second, outs, keep, give

    first, second, small, dmid_second, outs, keep, give = always(back)
    dproj_first, head_first, gains_first = first
    dproj_second, head_second, gains_second = second
    small_first, small_second = small

    def send_gradients():
        (packed,) = call(
            pack_kernel,
            "pack",
            [((SHARDS, own_rows, PACK), BF16)],
            head_first,
            head_second,
            small_first,
            small_second,
            gains_first,
            gains_second,
        )
        dproj_all = [dproj_first, exchange(dproj_second)]
        for ready in (dproj_all[1],):
            packed = after(packed, ready)
        return dproj_all, exchange(packed)

    dproj_all, packed = always(send_gradients)
    outs = send_along_x(outs, packed)

    def finish():
        input_grads = []
        for m in range(MICRO):
            rows = block((TPD, D), m, 0)
            input_grads += call(
                input_kernel,
                "input_grad",
                [((TPD, D), BF16)],
                dproj_all[m],
                rows_second,
                rows_second,
                block_input,
                (dmid_first, dmid_second)[m],
                attn_gain,
                specs={
                    1: block((SHARDS, own_rows, D), 0, 4, 0),
                    2: block((SHARDS, own_rows, D), 0, 5, 0),
                    3: rows,
                },
            )
        width = q_width + 2 * kv_width
        (owned,) = call(
            own_kernel,
            "own",
            [((own_rows, width + D + TPD), BF16)],
            packed,
            keep[0],
            permute(give, Y_SWAP)[0],
        )
        owned = exchange(owned.reshape(REPS, own_rows // REPS, -1), "rep")
        (share,) = call(
            share_kernel, "share", [(owned.shape, BF16)], owned
        )
        grad_qkv, grad_out, rest = call(
            last_kernel,
            "last",
            [((own_rows, width), F32), ((own_rows, D), F32), ((own_rows, TPD), F32)],
            exchange(share, "rep"),
            w_qkv,
            g_attn.astype(F32)[:, None],
        )
        four = HD // SHARDS
        return (
            jnp.concatenate(input_grads, axis=0),
            grad_qkv,
            grad_out,
            rest[:, HD : HD + EXPERTS],
            rest[:, 0],
            rest[:, HD + EXPERTS],
            rest[:four, HD + EXPERTS + 1],
            rest[:four, HD + EXPERTS + 2],
        )

    results = always(finish)
    outs = sum_along_x(outs, shard, results[0])
    came = permute(outs[1], Y_SWAP)
    grad_experts = widen(grad_experts)
    output = outs[0] + after(came, grad_experts[0]).astype(F32)
    output = (mid + output.reshape(mid.shape)).astype(BF16)
    return (output, *results, *grad_experts)


def solution(mesh):
    rows = P(("rep", "shard"), None)
    rep, split, vector = P("rep", None, None), P("shard", None), P("shard")
    expert = P("shard", None, None)
    return jax.shard_map(
        local,
        mesh=mesh,
        in_specs=(rows,) * 3 + (rep,) * 2 + (split,) * 3 + (vector,) * 4 + (expert,) * 3,
        out_specs=(rows,) * 2 + (split,) * 3 + (vector,) * 4 + (expert,) * 3,
        check_vma=False,
    )
```
